32 devices in a mesh: rep: 8 (over z, x), cp: 4 (over y, core).
Axes of the slice: x: 2, y: 2, z: 4, core: 2. Of those that a mesh axis runs over, the one named last changes fastest.
Arguments:
- tokens: bfloat16 [8192, 768], P(('rep', 'cp')), may hold values from -6 to 6
- cotangent: bfloat16 [8192, 768], P(('rep', 'cp')), may hold values from -6 to 6
- ln1_gain: bfloat16 [768], P('cp'), may hold values from 0.099609375 to 1.8984375
- ln1_bias: bfloat16 [768], P('cp'), may hold values from -3 to 3
- w_qkv: bfloat16 [768, 2304], P('cp'), may hold values from -0.21875 to 0.21875
- b_qv: bfloat16 [1536], P('cp'), may hold values from -3 to 3
- w_out: bfloat16 [768, 768], P('cp'), may hold values from -3 to 3
- b_out: bfloat16 [768], P('cp'), may hold values from -3 to 3
- ln2_gain: bfloat16 [768], P('cp'), may hold values from 0.099609375 to 1.8984375
- ln2_bias: bfloat16 [768], P('cp'), may hold values from -3 to 3
- w_in: bfloat16 [768, 3072], P('cp'), may hold values from -0.21875 to 0.21875
- b_in: bfloat16 [3072], P('cp'), may hold values from -3 to 3
- w_down: bfloat16 [3072, 768], P('cp'), may hold values from -0.109375 to 0.109375
- b_down: bfloat16 [768], P('cp'), may hold values from -3 to 3
Outputs:
- layer_out: bfloat16 [8192, 768], P(('rep', 'cp'))
- input_grad: bfloat16 [8192, 768], P(('rep', 'cp'))
- grad_ln1_gain: float32 [768], P('cp')
- grad_ln1_bias: float32 [768], P('cp')
- grad_w_qkv: float32 [768, 2304], P('cp')
- grad_b_qv: float32 [1536], P('cp')
- grad_w_out: float32 [768, 768], P('cp')
- grad_b_out: float32 [768], P('cp')
- grad_ln2_gain: float32 [768], P('cp')
- grad_ln2_bias: float32 [768], P('cp')
- grad_w_in: float32 [768, 3072], P('cp')
- grad_b_in: float32 [3072], P('cp')
- grad_w_down: float32 [3072, 768], P('cp')
- grad_b_down: float32 [768], P('cp')
The draws below stay inside these ranges and needn't reach their ends.
All inputs are finite; a program needn't handle non-finite values.
Results may differ from the reference program's by a relative error of at most 0.011.
Values may be sent and summed in bfloat16 or wider, within the bound.
A program may use at most 192 MiB of HBM per device.

```python
import jax
import jax.numpy as jnp
from jax import lax

D = 768
H = 12
HD = 64
FF = 3072
LENGTH = 1024
TOKENS = 8192
N_REP = 8


def block_scale(key, dims, split, low, largest):
    def one(position, blocks):
        draws = jax.random.uniform(jax.random.fold_in(jax.random.fold_in(key, 6), position), (blocks,), jnp.float32, low / len(split), largest / len(split))
        return jnp.repeat(jnp.exp(draws), dims[position] // blocks).reshape((-1,) + (1,) * (len(dims) - position - 1))

    factor_of = one(*split[0])
    for cut in split[1:]:
        factor_of = factor_of * one(*cut)
    return factor_of


def scatter_about(own_key, extent, width, reach, shards=(), held_as=jnp.bfloat16):
    drawn = jax.random.normal(own_key, extent, jnp.float32) * width
    if len(shards) > 0:
        drawn = block_scale(own_key, extent, shards, -0.22, 0.18) * drawn
    return jnp.clip(drawn, min=-reach, max=reach).astype(held_as)


def setup_inputs(seed: int = 0) -> dict:
    seeds = jax.random.split(jax.random.key(seed), 15)
    tokens = scatter_about(seeds[0], (TOKENS, D), 1.0, 6.0, ((0, 32),))
    cotangent = scatter_about(seeds[1], (TOKENS, D), 1.0, 6.0, ((0, 32),))
    ln1_gain = jnp.clip(1.0 + 0.18 * jax.random.normal(seeds[2], (D,), jnp.float32), 0.099609375, 1.8984375).astype(jnp.bfloat16)
    ln1_bias = scatter_about(seeds[3], (D,), 0.5, 3.0, ((0, 4),))
    w_qkv = scatter_about(seeds[4], (D, 3 * D), D ** -0.5, 0.21875, ((0, 4),))
    b_qv = scatter_about(seeds[5], (2 * D,), 0.5, 3.0, ((0, 4),))
    w_out = scatter_about(seeds[6], (D, D), (max(1, D // 192)) ** -0.5, 3.0, ((0, 4),))
    b_out = scatter_about(seeds[7], (D,), 0.5, 3.0, ((0, 4),))
    ln2_gain = jnp.clip(1.0 + 0.18 * jax.random.normal(seeds[8], (D,), jnp.float32), 0.099609375, 1.8984375).astype(jnp.bfloat16)
    ln2_bias = scatter_about(seeds[9], (D,), 0.5, 3.0, ((0, 4),))
    w_in = scatter_about(seeds[10], (D, FF), D ** -0.5, 0.21875, ((0, 4),))
    b_in = scatter_about(seeds[11], (FF,), 0.5, 3.0, ((0, 4),))
    w_down = scatter_about(seeds[12], (FF, D), FF ** -0.5, 0.109375, ((0, 4),))
    b_down = scatter_about(seeds[13], (D,), 0.5, 3.0, ((0, 4),))
    return {"tokens": tokens, "cotangent": cotangent, "ln1_gain": ln1_gain, "ln1_bias": ln1_bias, "w_qkv": w_qkv, "b_qv": b_qv, "w_out": w_out, "b_out": b_out, "ln2_gain": ln2_gain, "ln2_bias": ln2_bias, "w_in": w_in, "b_in": b_in, "w_down": w_down, "b_down": b_down}


@jax.custom_vjp
def low(v):
    return lax.optimization_barrier(v.astype(jnp.bfloat16)).astype(jnp.float32)

@jax.custom_vjp
def low_back(v):
    return v

def low_keep(v):
    return (low(v), None)

def low_pass(kept, grad):
    return (grad,)

def back_keep(v):
    return (v, None)

def back_low(kept, grad):
    return (low(grad),)
low.defvjp(low_keep, low_pass)
low_back.defvjp(back_keep, back_low)

def dot_high(left, right):
    return jnp.dot(left, right, precision=lax.Precision.HIGHEST)

def layer_norm(values, gain, shift):
    centred = values - lax.optimization_barrier(jnp.mean(values, axis=-1, keepdims=True))
    variance = lax.optimization_barrier(jnp.mean(centred * centred, axis=-1, keepdims=True))
    return centred * lax.rsqrt(variance + 1e-05) * gain + shift

def attend(query, keys, values):
    seq_length = query.shape[0]
    block_rows = min(512, seq_length)
    scale = HD ** (-0.5)
    key_places = jnp.arange(seq_length)

    def one_block(block_index):
        first_row = block_index * block_rows
        queries = lax.dynamic_slice_in_dim(query, first_row, block_rows, 0)
        scores = jnp.einsum('qhd,khd->hqk', queries, keys, precision=lax.Precision.HIGHEST) * scale
        scores = low_back(scores)
        allowed = (first_row + jnp.arange(block_rows))[:, None] >= key_places[None, :]
        scores = jnp.where(allowed[None], scores, -1e+30)
        weights = jax.nn.softmax(scores, axis=-1)
        return jnp.einsum('hqk,khd->qhd', weights, values, precision=lax.Precision.HIGHEST)
    blocks = lax.map(jax.checkpoint(one_block), jnp.arange(seq_length // block_rows))
    return blocks.reshape(seq_length, H * HD)

def layer(sequence, params):
    gain_one, shift_one, w_qkv, b_qv, w_out, b_out, gain_two, shift_two, w_in, b_in, w_down, b_down = params
    seq_length = sequence.shape[0]
    normed = low(layer_norm(sequence, gain_one, shift_one))
    mixed = dot_high(normed, w_qkv)
    query = low(low_back(mixed[:, :D] + b_qv[:D]))
    keys = low(low_back(mixed[:, D:2 * D]))
    values = low(low_back(mixed[:, 2 * D:] + b_qv[D:]))
    shape = (seq_length, H, HD)
    attended = low(low_back(attend(query.reshape(shape), keys.reshape(shape), values.reshape(shape))))
    branch = low_back(dot_high(attended, w_out) + b_out)
    middle = sequence + branch
    normed_two = low(layer_norm(middle, gain_two, shift_two))
    hidden = low_back(dot_high(normed_two, w_in) + b_in)
    active = low(jax.nn.gelu(hidden, approximate=True))
    return middle + dot_high(active, w_down) + b_down

def reference(tokens, cotangent, ln1_gain, ln1_bias, w_qkv, b_qv, w_out, b_out, ln2_gain, ln2_bias, w_in, b_in, w_down, b_down):
    params = tuple((item.astype(jnp.float32) for item in (ln1_gain, ln1_bias, w_qkv, b_qv, w_out, b_out, ln2_gain, ln2_bias, w_in, b_in, w_down, b_down)))
    inputs = tokens.astype(jnp.float32).reshape(N_REP, LENGTH, D)

    def forward(sequences, weights):
        return lax.map(lambda sequence: layer(sequence, weights), sequences)
    outputs, pullback = jax.vjp(forward, inputs, params)
    grad_inputs, grads = pullback(cotangent.astype(jnp.float32).reshape(N_REP, LENGTH, D))
    return (outputs.reshape(TOKENS, D).astype(jnp.bfloat16), grad_inputs.reshape(TOKENS, D).astype(jnp.bfloat16), grads[0], grads[1], grads[2], grads[3], grads[4], grads[5], grads[6], grads[7], grads[8], grads[9], grads[10], grads[11])
```

```python
from functools import partial

import jax
import jax.numpy as jnp
from jax import lax
from jax.experimental import pallas as pl
from jax.experimental.pallas import tpu as pltpu
from jax.sharding import PartitionSpec as P

D = 768
H = 12
HD = 64


def layer_norm(values, gain, shift):
    centred = values - jnp.mean(values, axis=-1, keepdims=True)
    variance = jnp.mean(centred * centred, axis=-1, keepdims=True)
    return centred * lax.rsqrt(variance + 1e-05) * gain + shift


def along_rows(left, right):
    return lax.dot_general(
        left, right, (((1,), (1,)), ((), ())), preferred_element_type=jnp.float32
    )


def across_rows(left, right):
    return lax.dot_general(
        left, right, (((0,), (0,)), ((), ())), preferred_element_type=jnp.float32
    )


def body(
    tokens,
    cotangent,
    ln1_gain,
    ln1_bias,
    w_qkv,
    b_qv,
    w_out,
    b_out,
    ln2_gain,
    ln2_bias,
    w_in,
    b_in,
    w_down,
    b_down,
):
    (
        gain_one,
        shift_one,
        qkv_full,
        qv_bias,
        out_full,
        out_bias,
        gain_two,
        shift_two,
        in_full,
        in_bias,
        down_full,
        down_bias,
    ) = (
        lax.all_gather(ln1_gain, "cp", axis=0, tiled=True),
        lax.all_gather(ln1_bias, "cp", axis=0, tiled=True),
        lax.all_gather(w_qkv, "cp", axis=0, tiled=True),
        lax.all_gather(b_qv, "cp", axis=0, tiled=True),
        lax.all_gather(w_out, "cp", axis=0, tiled=True),
        lax.all_gather(b_out, "cp", axis=0, tiled=True),
        lax.all_gather(ln2_gain, "cp", axis=0, tiled=True),
        lax.all_gather(ln2_bias, "cp", axis=0, tiled=True),
        lax.all_gather(w_in, "cp", axis=0, tiled=True),
        lax.all_gather(b_in, "cp", axis=0, tiled=True),
        lax.all_gather(w_down, "cp", axis=0, tiled=True),
        lax.all_gather(b_down, "cp", axis=0, tiled=True),
    )
    token_rows = tokens.shape[0]
    first_row = lax.axis_index("cp") * token_rows
    scale = HD ** (-0.5)
    query_places = first_row + jnp.arange(token_rows, dtype=jnp.int32)

    def allowed_mask(count):
        return (query_places[:, None] >= jnp.arange(count, dtype=jnp.int32)[None, :])[None]

    inputs = tokens.astype(jnp.float32)
    normed, norm_one_back = jax.vjp(
        layer_norm, inputs, gain_one.astype(jnp.float32), shift_one.astype(jnp.float32)
    )
    normed_low = normed.astype(jnp.bfloat16)
    mixed = jnp.dot(normed_low, qkv_full, preferred_element_type=jnp.float32)
    bias_float = qv_bias.astype(jnp.float32)
    query = (mixed[:, :D] + bias_float[:D]).astype(jnp.bfloat16)
    keys = mixed[:, D : 2 * D].astype(jnp.bfloat16)
    values = (mixed[:, 2 * D :] + bias_float[D:]).astype(jnp.bfloat16)
    query_heads = query.reshape(token_rows, H, HD)
    weighted = jnp.zeros((token_rows, H, HD), jnp.float32)
    running_top = jnp.full((H, token_rows), -1e30, jnp.float32)
    key_piece = lax.all_gather(keys, "cp", axis=0, tiled=True)
    value_piece = lax.all_gather(values, "cp", axis=0, tiled=True)
    count = key_piece.shape[0]
    key_heads = key_piece.reshape(count, H, HD)
    value_heads = value_piece.astype(jnp.float32).reshape(count, H, HD)
    allowed = allowed_mask(count)
    scores = (
        jnp.einsum("qhd,khd->hqk", query_heads, key_heads, preferred_element_type=jnp.float32)
        * scale
    )
    scores = jnp.where(allowed, scores, -1e30)
    new_top = jnp.maximum(running_top, jnp.max(scores, axis=-1))
    factor = jnp.exp(running_top - new_top)
    probs = jnp.where(allowed, jnp.exp(scores - new_top[..., None]), 0.0)
    running_total = jnp.sum(probs, axis=-1)
    update = jnp.einsum("hqk,khd->qhd", probs, value_heads, precision=lax.Precision.HIGHEST)
    weighted = weighted * factor.T[..., None] + update
    weighted, running_top, running_total = (weighted, new_top, running_total)
    out_exact = weighted / running_total.T[..., None]
    logsum = running_top + jnp.log(running_total)
    attended_low = out_exact.reshape(token_rows, D).astype(jnp.bfloat16)
    middle = inputs + (
        jnp.dot(attended_low, out_full, preferred_element_type=jnp.float32)
        + out_bias.astype(jnp.float32)
    )
    normed_two, norm_two_back = jax.vjp(
        layer_norm, middle, gain_two.astype(jnp.float32), shift_two.astype(jnp.float32)
    )
    normed_two_low = normed_two.astype(jnp.bfloat16)
    hidden = jnp.dot(normed_two_low, in_full, preferred_element_type=jnp.float32) + in_bias.astype(
        jnp.float32
    )
    active, gelu_back = jax.vjp(partial(jax.nn.gelu, approximate=True), hidden)
    active_low = active.astype(jnp.bfloat16)
    result = (
        middle
        + jnp.dot(active_low, down_full, preferred_element_type=jnp.float32)
        + down_bias.astype(jnp.float32)
    )
    layer_out = result.astype(jnp.bfloat16)
    qkv_back, out_back, in_back, down_back = (
        lax.all_gather(w_qkv, "cp", axis=0, tiled=True),
        lax.all_gather(w_out, "cp", axis=0, tiled=True),
        lax.all_gather(w_in, "cp", axis=0, tiled=True),
        lax.all_gather(w_down, "cp", axis=0, tiled=True),
    )
    grad_output = cotangent.astype(jnp.float32)
    grad_down = across_rows(active_low, cotangent)
    grad_down_bias = jnp.sum(grad_output, axis=0)
    grad_active = along_rows(cotangent, down_back)
    grad_hidden = gelu_back(grad_active)[0].astype(jnp.bfloat16)
    grad_in = across_rows(normed_two_low, grad_hidden)
    grad_in_bias = jnp.sum(grad_hidden.astype(jnp.float32), axis=0)
    grad_middle_part, grad_gain_two, grad_shift_two = norm_two_back(
        along_rows(grad_hidden, in_back)
    )
    grad_middle = grad_output + grad_middle_part
    grad_branch = grad_middle.astype(jnp.bfloat16)
    grad_out_proj = across_rows(attended_low, grad_branch)
    grad_out_bias = jnp.sum(grad_branch.astype(jnp.float32), axis=0)
    grad_attended = along_rows(grad_branch, out_back).astype(jnp.bfloat16)
    grad_heads = grad_attended.reshape(token_rows, H, HD)
    grad_heads_float = grad_heads.astype(jnp.float32)
    delta = jnp.einsum("qhd,qhd->hq", grad_heads_float, out_exact)
    key_piece = lax.all_gather(keys, "cp", axis=0, tiled=True)
    value_piece = lax.all_gather(values, "cp", axis=0, tiled=True)
    count = key_piece.shape[0]
    key_heads = key_piece.reshape(count, H, HD)
    value_heads = value_piece.reshape(count, H, HD)
    allowed = allowed_mask(count)
    scores = (
        jnp.einsum("qhd,khd->hqk", query_heads, key_heads, preferred_element_type=jnp.float32)
        * scale
    )
    probs = jnp.where(allowed, jnp.exp(scores - logsum[..., None]), 0.0)
    grad_probs = jnp.einsum(
        "qhd,khd->hqk", grad_heads, value_heads, preferred_element_type=jnp.float32
    )
    grad_scores = (probs * (grad_probs - delta[..., None])).astype(jnp.bfloat16)
    grad_query = jnp.einsum(
        "hqk,khd->qhd", grad_scores, key_heads, preferred_element_type=jnp.float32
    )
    paired = jnp.concatenate([keys, values], axis=1)
    piece = lax.all_gather(paired, "cp", axis=0, tiled=True)
    count = piece.shape[0]
    key_heads = piece[:, :D].reshape(count, H, HD)
    value_heads = piece[:, D:].reshape(count, H, HD)
    allowed = allowed_mask(count)
    scores = (
        jnp.einsum("qhd,khd->hqk", query_heads, key_heads, preferred_element_type=jnp.float32)
        * scale
    )
    probs = jnp.where(allowed, jnp.exp(scores - logsum[..., None]), 0.0)
    grad_probs = jnp.einsum(
        "qhd,khd->hqk", grad_heads, value_heads, preferred_element_type=jnp.float32
    )
    grad_scores = (probs * (grad_probs - delta[..., None])).astype(jnp.bfloat16)
    key_term = (
        jnp.einsum(
            "hqk,qhd->khd", grad_scores, query_heads, preferred_element_type=jnp.float32
        ).reshape(count, D)
        * scale
    )
    value_term = jnp.einsum(
        "hqk,qhd->khd", probs, grad_heads_float, precision=lax.Precision.HIGHEST
    ).reshape(count, D)
    terms = jnp.concatenate([key_term, value_term], axis=1)
    owned_terms = lax.psum_scatter(terms, "cp", scatter_dimension=0, tiled=True)
    grad_keys = owned_terms[:, :D]
    grad_values = owned_terms[:, D:]
    grad_query_low = (grad_query * scale).reshape(token_rows, D).astype(jnp.bfloat16)
    grad_mixed = jnp.concatenate(
        [grad_query_low, grad_keys.astype(jnp.bfloat16), grad_values.astype(jnp.bfloat16)], axis=1
    )
    grad_qkv = across_rows(normed_low, grad_mixed)
    mixed_sums = jnp.sum(grad_mixed.astype(jnp.float32), axis=0)
    grad_qv_bias = jnp.concatenate([mixed_sums[:D], mixed_sums[2 * D :]])
    grad_input_part, grad_gain_one, grad_shift_one = norm_one_back(along_rows(grad_mixed, qkv_back))
    input_grad = (grad_middle + grad_input_part).astype(jnp.bfloat16)
    owned = (
        lax.psum_scatter(grad_gain_one, "cp", scatter_dimension=0, tiled=True),
        lax.psum_scatter(grad_shift_one, "cp", scatter_dimension=0, tiled=True),
        lax.psum_scatter(grad_qkv, "cp", scatter_dimension=0, tiled=True),
        lax.psum_scatter(grad_qv_bias, "cp", scatter_dimension=0, tiled=True),
        lax.psum_scatter(grad_out_proj, "cp", scatter_dimension=0, tiled=True),
        lax.psum_scatter(grad_out_bias, "cp", scatter_dimension=0, tiled=True),
        lax.psum_scatter(grad_gain_two, "cp", scatter_dimension=0, tiled=True),
        lax.psum_scatter(grad_shift_two, "cp", scatter_dimension=0, tiled=True),
        lax.psum_scatter(grad_in, "cp", scatter_dimension=0, tiled=True),
        lax.psum_scatter(grad_in_bias, "cp", scatter_dimension=0, tiled=True),
        lax.psum_scatter(grad_down, "cp", scatter_dimension=0, tiled=True),
        lax.psum_scatter(grad_down_bias, "cp", scatter_dimension=0, tiled=True),
    )
    totals = lax.psum(
        (
            owned[0],
            owned[1],
            owned[2],
            owned[3],
            owned[4],
            owned[5],
            owned[6],
            owned[7],
            owned[8],
            owned[9],
            owned[10],
            owned[11],
        ),
        "rep",
    )
    return (layer_out, input_grad) + tuple(totals)


BF = jnp.bfloat16
F32 = jnp.float32
MESH = pl.DeviceIdType.MESH
VM = pl.BlockSpec(memory_space=pltpu.VMEM)
CHUNKS = 4


def params(collective_id=None, **more):
    if collective_id is not None:
        more.update(collective_id=collective_id, has_side_effects=True)
    return pltpu.CompilerParams(vmem_limit_bytes=48 * 2**20, **more)


def places():
    me = lax.axis_index("cp")
    core = lax.rem(me, 2)
    row = me // 2
    return me, row * 2 + 1 - core, (1 - row) * 2 + core, (1 - row) * 2 + 1 - core


def greet(*others):
    barrier = pltpu.get_barrier_semaphore()
    for other in others:
        pl.semaphore_signal(barrier, inc=1, device_id={"cp": other}, device_id_type=MESH)
    pl.semaphore_wait(barrier, len(others))


def push(src, dst, send, recv, other):
    return pltpu.make_async_remote_copy(
        src_ref=src, dst_ref=dst, send_sem=send, recv_sem=recv,
        device_id={"cp": other}, device_id_type=MESH,
    )


def open_kernel(x_ref, w_ref, s_ref, xa_ref, wa_ref, sa_ref, send, recv):
    me, sib, opp, diag = places()
    greet(sib, opp, diag)
    part = x_ref.shape[0] // CHUNKS
    pieces = [pl.ds(k * part, part) for k in range(CHUNKS)]
    across = [
        push(x_ref.at[p], xa_ref.at[me, p], send.at[k], recv.at[k], opp)
        for k, p in enumerate(pieces)
    ]
    slot = CHUNKS
    rest = []
    for other in (opp, diag, sib):
        rest.append(push(s_ref, sa_ref.at[me], send.at[slot], recv.at[slot], other))
        rest.append(push(w_ref.at[other], wa_ref.at[me], send.at[slot + 1], recv.at[slot + 1], other))
        slot += 2
    rest.append(push(x_ref, xa_ref.at[me], send.at[slot], recv.at[slot], sib))
    slot += 1
    for copy in across + rest:
        copy.start()
    xa_ref[me] = x_ref[...]
    wa_ref[me] = w_ref[me]
    sa_ref[me] = s_ref[...]
    onward = []
    for k, p in enumerate(pieces):
        across[k].wait_recv()
        copy = push(xa_ref.at[opp, p], xa_ref.at[opp, p], send.at[slot + k], recv.at[slot + k], sib)
        copy.start()
        onward.append(copy)
    for copy in across:
        copy.wait_send()
    for copy in rest + onward:
        copy.wait()


def open_exchange(x, w, s):
    n = w.shape[0]
    count = 2 * CHUNKS + 7
    return pl.pallas_call(
        open_kernel,
        out_shape=[
            jax.ShapeDtypeStruct((n,) + x.shape, x.dtype),
            jax.ShapeDtypeStruct(w.shape, w.dtype),
            jax.ShapeDtypeStruct((n,) + s.shape, s.dtype),
        ],
        in_specs=[VM] * 3,
        out_specs=[VM] * 3,
        scratch_shapes=[pltpu.SemaphoreType.DMA((count,))] * 2,
        compiler_params=params(0),
        name="open_exchange",
    )(x, w, s)


def swap_kernel(w_ref, wa_ref, send, recv):
    me, sib, opp, diag = places()
    greet(sib, opp, diag)
    copies = []
    for k, other in enumerate((opp, diag, sib)):
        copies.append(push(w_ref.at[other], wa_ref.at[me], send.at[k], recv.at[k], other))
        copies[-1].start()
    wa_ref[me] = w_ref[me]
    for copy in copies:
        copy.wait()


def swap(w, collective_id):
    return pl.pallas_call(
        swap_kernel,
        out_shape=jax.ShapeDtypeStruct(w.shape, w.dtype),
        in_specs=[VM],
        out_specs=VM,
        scratch_shapes=[pltpu.SemaphoreType.DMA((3,))] * 2,
        compiler_params=params(collective_id),
        name="swap",
    )(w)


class Reduce:
    def __init__(self, p_ref, near, sent, far, send, recv):
        self.me, self.sib, self.opp, self.diag = places()
        self.refs = (p_ref, near, sent, far)
        self.part = part = p_ref.shape[1] // CHUNKS
        self.pieces = [pl.ds(k * part, part) for k in range(CHUNKS)]
        self.first, self.own, self.across = [], [], []
        for k, p in enumerate(self.pieces):
            self.first.append(push(p_ref.at[self.diag, p], near.at[0, p], send.at[k], recv.at[k], self.sib))
            self.own.append(push(p_ref.at[self.sib, p], near.at[1, p], send.at[CHUNKS + k], recv.at[CHUNKS + k], self.sib))
            self.across.append(push(sent.at[p], far.at[p], send.at[2 * CHUNKS + k], recv.at[2 * CHUNKS + k], self.opp))

    def start(self):
        p_ref, near, sent, far = self.refs
        for copy in self.first + self.own:
            copy.start()
        for k, p in enumerate(self.pieces):
            self.first[k].wait_recv()
            sent[p] = (p_ref[self.opp, p].astype(F32) + near[0, p].astype(F32)).astype(BF)
            self.across[k].start()

    def piece(self, k):
        p_ref, near, sent, far = self.refs
        p = self.pieces[k]
        self.own[k].wait_recv()
        self.across[k].wait_recv()
        return p_ref[self.me, p].astype(F32) + near[1, p].astype(F32) + far[p].astype(F32)

    def finish(self):
        for copy in self.first + self.own + self.across:
            copy.wait_send()


class Gather:
    def __init__(self, x_ref, all_ref, send, recv, base):
        self.me, self.sib, self.opp, self.diag = places()
        part = x_ref.shape[0] // CHUNKS
        self.pieces = [pl.ds(k * part, part) for k in range(CHUNKS)]
        self.across, self.near, self.onward = [], [], []
        me, sib, opp = self.me, self.sib, self.opp
        for k, p in enumerate(self.pieces):
            a, b, c = base + k, base + CHUNKS + k, base + 2 * CHUNKS + k
            self.across.append(push(x_ref.at[p], all_ref.at[me, p], send.at[a], recv.at[a], opp))
            self.near.append(push(x_ref.at[p], all_ref.at[me, p], send.at[b], recv.at[b], sib))
            self.onward.append(push(all_ref.at[opp, p], all_ref.at[opp, p], send.at[c], recv.at[c], sib))

    def start(self, k):
        self.across[k].start()
        self.near[k].start()

    def finish(self):
        for k in range(CHUNKS):
            self.across[k].wait_recv()
            self.onward[k].start()
        for copy in self.across:
            copy.wait_send()
        for copy in self.near + self.onward:
            copy.wait()


def normalise(values):
    centred = values - jnp.mean(values, axis=-1, keepdims=True)
    variance = jnp.mean(centred * centred, axis=-1, keepdims=True)
    scale = lax.rsqrt(variance + 1e-05)
    return centred * scale, scale


def norm_back(upstream, gain, unit, scale):
    inner = upstream * gain
    return scale * (
        inner
        - jnp.mean(inner, axis=-1, keepdims=True)
        - unit * jnp.mean(inner * unit, axis=-1, keepdims=True)
    )


def middle_kernel(p_ref, x_ref, vec_ref, r_ref, all_ref, near, sent, far, mine, send, recv):
    me, sib, opp, diag = places()
    greet(sib, opp)
    reduce = Reduce(p_ref, near, sent, far, send, recv)
    gather = Gather(mine, all_ref, send, recv, 3 * CHUNKS)
    reduce.start()
    for k, p in enumerate(reduce.pieces):
        r = x_ref[p].astype(F32) + (reduce.piece(k) + vec_ref[0:1])
        r_ref[p] = r
        unit, _ = normalise(r)
        low = (unit * vec_ref[1:2] + vec_ref[2:3]).astype(BF)
        mine[p] = low
        gather.start(k)
        all_ref[me, p] = low
    gather.finish()
    reduce.finish()


def reduce_scratch(rows, wide):
    return [
        pltpu.VMEM((2, rows, wide), BF),
        pltpu.VMEM((rows, wide), BF),
        pltpu.VMEM((rows, wide), BF),
    ]


def middle_step(p, x, vec):
    n, rows, wide = p.shape
    return pl.pallas_call(
        middle_kernel,
        out_shape=[
            jax.ShapeDtypeStruct((rows, wide), F32),
            jax.ShapeDtypeStruct((n, rows, wide), BF),
        ],
        in_specs=[VM] * 3,
        out_specs=[VM] * 2,
        scratch_shapes=reduce_scratch(rows, wide)
        + [pltpu.VMEM((rows, wide), BF)]
        + [pltpu.SemaphoreType.DMA((6 * CHUNKS,))] * 2,
        compiler_params=params(1),
        name="middle_step",
    )(p, x, vec)


def back_kernel(p_ref, r_ref, g_ref, vec_ref, gr_ref, all_ref, sums_ref, near, sent, far, mine, send, recv):
    me, sib, opp, diag = places()
    greet(sib, opp)
    reduce = Reduce(p_ref, near, sent, far, send, recv)
    gather = Gather(mine, all_ref, send, recv, 3 * CHUNKS)
    reduce.start()
    sums_ref[...] = jnp.zeros_like(sums_ref)
    for k, p in enumerate(reduce.pieces):
        unit, scale = normalise(r_ref[p])
        g = g_ref[p].astype(F32)
        upstream = reduce.piece(k)
        gr = g + norm_back(upstream, vec_ref[1:2], unit, scale)
        gr_ref[p] = gr
        low = gr.astype(BF)
        mine[p] = low
        gather.start(k)
        all_ref[me, p] = low
        sums_ref[0:1] += jnp.sum(upstream * unit, axis=0, keepdims=True)
        sums_ref[1:2] += jnp.sum(upstream, axis=0, keepdims=True)
        sums_ref[2:3] += jnp.sum(low.astype(F32), axis=0, keepdims=True)
        sums_ref[3:4] += jnp.sum(g, axis=0, keepdims=True)
    gather.finish()
    reduce.finish()


def back_step(p, r, g, vec):
    n, rows, wide = p.shape
    return pl.pallas_call(
        back_kernel,
        out_shape=[
            jax.ShapeDtypeStruct((rows, wide), F32),
            jax.ShapeDtypeStruct((n, rows, wide), BF),
            jax.ShapeDtypeStruct((8, wide), F32),
        ],
        in_specs=[VM] * 4,
        out_specs=[VM] * 3,
        scratch_shapes=reduce_scratch(rows, wide)
        + [pltpu.VMEM((rows, wide), BF)]
        + [pltpu.SemaphoreType.DMA((6 * CHUNKS,))] * 2,
        compiler_params=params(2),
        name="back_step",
    )(p, r, g, vec)


def last_kernel(p_ref, x_ref, gr_ref, vec_ref, out_ref, sums_ref, near, sent, far, send, recv):
    me, sib, opp, diag = places()
    greet(sib, opp)
    reduce = Reduce(p_ref, near, sent, far, send, recv)
    reduce.start()
    sums_ref[...] = jnp.zeros_like(sums_ref)
    for k, p in enumerate(reduce.pieces):
        unit, scale = normalise(x_ref[p].astype(F32))
        upstream = reduce.piece(k)
        out_ref[p] = (gr_ref[p] + norm_back(upstream, vec_ref[0:1], unit, scale)).astype(BF)
        sums_ref[0:1] += jnp.sum(upstream * unit, axis=0, keepdims=True)
        sums_ref[1:2] += jnp.sum(upstream, axis=0, keepdims=True)
    reduce.finish()


def last_step(p, x, gr, vec):
    n, rows, wide = p.shape
    return pl.pallas_call(
        last_kernel,
        out_shape=[
            jax.ShapeDtypeStruct((rows, wide), BF),
            jax.ShapeDtypeStruct((8, wide), F32),
        ],
        in_specs=[VM] * 4,
        out_specs=[VM] * 2,
        scratch_shapes=reduce_scratch(rows, wide)
        + [pltpu.SemaphoreType.DMA((3 * CHUNKS,))] * 2,
        compiler_params=params(3),
        name="last_step",
    )(p, x, gr, vec)


def head_mask(wide):
    lane = lax.broadcasted_iota(jnp.int32, (1, wide), 1)
    low = pl.program_id(0) * HD
    return (lane >= low) & (lane < low + HD)


def causal(block, first, count):
    row = lax.broadcasted_iota(jnp.int32, (block, count), 0) + first
    return row >= lax.broadcasted_iota(jnp.int32, (block, count), 1)


def attend_kernel(block, q_ref, k_ref, v_ref, o_ref, lse_ref):
    length, wide = q_ref.shape
    mask = head_mask(wide)
    for first in range(0, length, block):
        count = first + block
        rows = slice(first, count)
        q = jnp.where(mask, q_ref[rows], 0) * BF(HD**-0.5)
        s = jnp.where(causal(block, first, count), along_rows(q, k_ref[:count]), -1e30)
        top = jnp.max(s, axis=-1, keepdims=True)
        p = jnp.exp(s - top)
        total = jnp.sum(p, axis=-1, keepdims=True)
        o = jnp.dot(p.astype(BF), v_ref[:count], preferred_element_type=F32) / total
        o_ref[rows] = jnp.where(mask, o.astype(BF), o_ref[rows])
        lse_ref[0, rows] = jnp.broadcast_to(top + jnp.log(total), (block, 128))


def attend(q, k, v):
    length, wide = q.shape
    heads = wide // HD
    whole = pl.BlockSpec((length, wide), lambda h: (0, 0))
    return pl.pallas_call(
        partial(attend_kernel, min(256, length)),
        grid=(heads,),
        out_shape=[
            jax.ShapeDtypeStruct((length, wide), BF),
            jax.ShapeDtypeStruct((heads, length, 128), F32),
        ],
        in_specs=[whole] * 3,
        out_specs=[whole, pl.BlockSpec((1, length, 128), lambda h: (h, 0, 0))],
        compiler_params=params(),
        cost_estimate=pl.CostEstimate(flops=4 * heads * length * length * 256, bytes_accessed=8 * length * wide, transcendentals=heads * length * length),
        name="attend",
    )(q, k, v)


def attend_back_kernel(block, q_ref, k_ref, v_ref, go_ref, lse_ref, gq_ref, gk_ref, gv_ref, gk_sum, gv_sum):
    length, wide = q_ref.shape
    mask = head_mask(wide)

    @pl.when(pl.program_id(0) == 0)
    def _():
        gk_sum[...] = jnp.zeros_like(gk_sum)
        gv_sum[...] = jnp.zeros_like(gv_sum)

    for first in range(0, length, block):
        count = first + block
        rows = slice(first, count)
        q = jnp.where(mask, q_ref[rows], 0) * BF(HD**-0.5)
        go = jnp.where(mask, go_ref[rows], 0)
        s = along_rows(q, k_ref[:count])
        p = jnp.where(causal(block, first, count), jnp.exp(s - lse_ref[0, rows, 0:1]), 0.0)
        dp = along_rows(go, v_ref[:count])
        delta = jnp.sum(p * dp, axis=-1, keepdims=True)
        ds = (p * (dp - delta)).astype(BF)
        gq = jnp.dot(ds, k_ref[:count], preferred_element_type=F32) * HD**-0.5
        gq_ref[rows] = jnp.where(mask, gq.astype(BF), gq_ref[rows])
        gk_sum[:count] += across_rows(ds, q)
        gv_sum[:count] += across_rows(p.astype(BF), go)

    @pl.when(pl.program_id(0) == pl.num_programs(0) - 1)
    def _():
        gk_ref[...] = gk_sum[...].astype(BF)
        gv_ref[...] = gv_sum[...].astype(BF)


def attend_back(q, k, v, go, lse):
    length, wide = q.shape
    heads = wide // HD
    whole = pl.BlockSpec((length, wide), lambda h: (0, 0))
    return pl.pallas_call(
        partial(attend_back_kernel, min(256, length)),
        grid=(heads,),
        out_shape=[jax.ShapeDtypeStruct((length, wide), BF)] * 3,
        in_specs=[whole] * 4 + [pl.BlockSpec((1, length, 128), lambda h: (h, 0, 0))],
        out_specs=[whole] * 3,
        scratch_shapes=[pltpu.VMEM((length, wide), F32)] * 2,
        compiler_params=params(),
        cost_estimate=pl.CostEstimate(flops=10 * heads * length * length * 256, bytes_accessed=16 * length * wide, transcendentals=heads * length * length),
        name="attend_back",
    )(q, k, v, go, lse)


def turn(blocks, n):
    me = lax.axis_index("cp")
    result = jnp.zeros_like(blocks)
    result = lax.dynamic_update_index_in_dim(result, lax.dynamic_index_in_dim(blocks, me, 0), me, 0)
    for step in range(1, n):
        there, back = lax.rem(me + step, n), lax.rem(me + n - step, n)
        got = lax.ppermute(
            lax.dynamic_index_in_dim(blocks, there, 0), "cp", [(i, (i + step) % n) for i in range(n)]
        )
        result = lax.dynamic_update_index_in_dim(result, got, back, 0)
    return result


def head_body(
    tokens, cotangent, ln1_gain, ln1_bias, w_qkv, b_qv, w_out, b_out,
    ln2_gain, ln2_bias, w_in, b_in, w_down, b_down, *, n,
):
    rows = tokens.shape[0]
    length = rows * n
    me = lax.axis_index("cp")
    share = D // n
    ff_share = w_in.shape[1] // n
    tidy = jnp.concatenate([ln1_gain, ln1_bias, b_out, ln2_gain, ln2_bias, b_down, b_qv])
    tidy = jnp.concatenate([tidy, jnp.zeros((-tidy.shape[0] % 2048,), BF)]).reshape(-1, 128)
    w_blocks = w_qkv.reshape(share, 3, n, share).transpose(2, 0, 1, 3).reshape(n, share, 3 * share)
    in_cols = turn(w_in.reshape(share, n, ff_share).transpose(1, 0, 2), n).reshape(D, ff_share)
    cot_all = lax.all_gather(cotangent, "cp", axis=0, tiled=True)
    x_all, w_mine, tidy_all = open_exchange(tokens, w_blocks, tidy)
    w_mine = w_mine.reshape(D, 3 * share)
    tidy_all = tidy_all.reshape(n, -1).astype(F32)
    gain_one, shift_one, out_bias, gain_two, shift_two, down_bias = (
        tidy_all[:, i * share : (i + 1) * share].reshape(D) for i in range(6)
    )
    qv_bias = tidy_all[:, 6 * share : 8 * share].reshape(2, D)
    qv_mine = lax.dynamic_slice_in_dim(qv_bias, me * share, share, 1)
    vec_two = jnp.concatenate([jnp.stack([out_bias, gain_two, shift_two]), jnp.zeros((5, D), F32)])
    vec_one = jnp.concatenate([gain_one[None], jnp.zeros((7, D), F32)])

    n1 = layer_norm(x_all.reshape(length, D).astype(F32), gain_one, shift_one).astype(BF)
    mixed = jnp.dot(n1, w_mine, preferred_element_type=F32)
    q = (mixed[:, :share] + qv_mine[0]).astype(BF)
    k = mixed[:, share : 2 * share].astype(BF)
    v = (mixed[:, 2 * share :] + qv_mine[1]).astype(BF)
    o, lse = attend(q, k, v)
    o_part = jnp.dot(o, w_out, preferred_element_type=F32).astype(BF).reshape(n, rows, D)
    r, n2 = middle_step(o_part, tokens, vec_two)
    n2 = n2.reshape(length, D)
    hidden = jnp.dot(n2, in_cols, preferred_element_type=F32) + b_in.astype(F32)
    active, gelu_back = jax.vjp(partial(jax.nn.gelu, approximate=True), hidden)
    a = active.astype(BF)
    y_part = jnp.dot(a, w_down, preferred_element_type=F32).astype(BF)
    y = lax.psum_scatter(y_part, "cp", scatter_dimension=0, tiled=True)
    layer_out = (r + y.astype(F32) + down_bias).astype(BF)

    gu = gelu_back(along_rows(cot_all, w_down))[0].astype(BF)
    n2_part = along_rows(gu, in_cols).astype(BF).reshape(n, rows, D)
    grad_down = across_rows(a, cot_all).astype(BF)
    grad_in = turn(across_rows(n2, gu).astype(BF).reshape(n, share, ff_share), n)
    grad_in = grad_in.transpose(1, 0, 2).reshape(share, n * ff_share)
    grad_in_bias = jnp.sum(gu.astype(F32), axis=0)
    grad_down = lax.psum(grad_down, "rep").astype(F32)
    grad_in = lax.psum(grad_in, "rep").astype(F32)

    gr, gz, sums_two = back_step(n2_part, r, cotangent, vec_two)
    gz = gz.reshape(length, D)
    go = along_rows(gz, w_out).astype(BF)
    grad_out = lax.psum(across_rows(o, gz).astype(BF), "rep").astype(F32)
    gq, gk, gv = attend_back(q, k, v, go, lse)
    gm = jnp.concatenate([gq, gk, gv], axis=1)
    grad_qkv = swap(across_rows(n1, gm).astype(BF).reshape(n, share, 3 * share), 4)
    grad_qkv = grad_qkv.reshape(n, share, 3, share).transpose(1, 2, 0, 3).reshape(share, 3 * D)
    grad_qkv = lax.psum(grad_qkv, "rep").astype(F32)
    n1_part = along_rows(gm, w_mine).astype(BF).reshape(n, rows, D)
    input_grad, sums_one = last_step(n1_part, tokens, gr, vec_one)

    qv_sums = jnp.zeros((2, D), F32)
    qv_sums = lax.dynamic_update_slice(
        qv_sums,
        jnp.stack([jnp.sum(gq.astype(F32), axis=0), jnp.sum(gv.astype(F32), axis=0)]),
        (0, me * share),
    )
    in_sums = lax.dynamic_update_slice(jnp.zeros((n * ff_share,), F32), grad_in_bias, (me * ff_share,))
    sums = lax.psum(
        jnp.concatenate([sums_one[:2], sums_two[:4], qv_sums, in_sums.reshape(-1, D)]), ("rep", "cp")
    )
    own = lax.dynamic_slice_in_dim(sums[:6], me * share, share, 1)
    own_qv = lax.dynamic_slice_in_dim(sums[6:8].reshape(-1), me * 2 * share, 2 * share, 0)
    own_in = lax.dynamic_slice_in_dim(sums[8:].reshape(-1), me * ff_share, ff_share, 0)
    return (
        layer_out, input_grad, own[0], own[1], grad_qkv, own_qv, grad_out, own[4],
        own[2], own[3], grad_in, own_in, grad_down, own[5],
    )


def solution(mesh):
    placed = (
        P(("rep", "cp"), None),
        P(("rep", "cp"), None),
        P("cp"),
        P("cp"),
        P("cp", None),
        P("cp"),
        P("cp", None),
        P("cp"),
        P("cp"),
        P("cp"),
        P("cp", None),
        P("cp"),
        P("cp", None),
        P("cp"),
    )
    count = mesh.shape["cp"]
    by_heads = count == 4 and H % count == 0
    return jax.shard_map(
        partial(head_body, n=count) if by_heads else body,
        mesh=mesh,
        in_specs=placed,
        out_specs=(
            P(("rep", "cp"), None),
            P(("rep", "cp"), None),
            P("cp"),
            P("cp"),
            P("cp", None),
            P("cp"),
            P("cp", None),
            P("cp"),
            P("cp"),
            P("cp"),
            P("cp", None),
            P("cp"),
            P("cp", None),
            P("cp"),
        ),
        check_vma=False,
    )
```

```python
from functools import partial

import jax
import jax.numpy as jnp
from jax import lax
from jax.experimental import pallas as pl
from jax.experimental.pallas import tpu as pltpu
from jax.sharding import PartitionSpec as P

D = 768
H = 12
HD = 64


def layer_norm(values, gain, shift):
    centred = values - jnp.mean(values, axis=-1, keepdims=True)
    variance = jnp.mean(centred * centred, axis=-1, keepdims=True)
    return centred * lax.rsqrt(variance + 1e-05) * gain + shift


def along_rows(left, right):
    return lax.dot_general(
        left, right, (((1,), (1,)), ((), ())), preferred_element_type=jnp.float32
    )


def across_rows(left, right):
    return lax.dot_general(
        left, right, (((0,), (0,)), ((), ())), preferred_element_type=jnp.float32
    )


def body(
    tokens,
    cotangent,
    ln1_gain,
    ln1_bias,
    w_qkv,
    b_qv,
    w_out,
    b_out,
    ln2_gain,
    ln2_bias,
    w_in,
    b_in,
    w_down,
    b_down,
):
    (
        gain_one,
        shift_one,
        qkv_full,
        qv_bias,
        out_full,
        out_bias,
        gain_two,
        shift_two,
        in_full,
        in_bias,
        down_full,
        down_bias,
    ) = (
        lax.all_gather(ln1_gain, "cp", axis=0, tiled=True),
        lax.all_gather(ln1_bias, "cp", axis=0, tiled=True),
        lax.all_gather(w_qkv, "cp", axis=0, tiled=True),
        lax.all_gather(b_qv, "cp", axis=0, tiled=True),
        lax.all_gather(w_out, "cp", axis=0, tiled=True),
        lax.all_gather(b_out, "cp", axis=0, tiled=True),
        lax.all_gather(ln2_gain, "cp", axis=0, tiled=True),
        lax.all_gather(ln2_bias, "cp", axis=0, tiled=True),
        lax.all_gather(w_in, "cp", axis=0, tiled=True),
        lax.all_gather(b_in, "cp", axis=0, tiled=True),
        lax.all_gather(w_down, "cp", axis=0, tiled=True),
        lax.all_gather(b_down, "cp", axis=0, tiled=True),
    )
    token_rows = tokens.shape[0]
    first_row = lax.axis_index("cp") * token_rows
    scale = HD ** (-0.5)
    query_places = first_row + jnp.arange(token_rows, dtype=jnp.int32)

    def allowed_mask(count):
        return (query_places[:, None] >= jnp.arange(count, dtype=jnp.int32)[None, :])[None]

    inputs = tokens.astype(jnp.float32)
    normed, norm_one_back = jax.vjp(
        layer_norm, inputs, gain_one.astype(jnp.float32), shift_one.astype(jnp.float32)
    )
    normed_low = normed.astype(jnp.bfloat16)
    mixed = jnp.dot(normed_low, qkv_full, preferred_element_type=jnp.float32)
    bias_float = qv_bias.astype(jnp.float32)
    query = (mixed[:, :D] + bias_float[:D]).astype(jnp.bfloat16)
    keys = mixed[:, D : 2 * D].astype(jnp.bfloat16)
    values = (mixed[:, 2 * D :] + bias_float[D:]).astype(jnp.bfloat16)
    query_heads = query.reshape(token_rows, H, HD)
    weighted = jnp.zeros((token_rows, H, HD), jnp.float32)
    running_top = jnp.full((H, token_rows), -1e30, jnp.float32)
    key_piece = lax.all_gather(keys, "cp", axis=0, tiled=True)
    value_piece = lax.all_gather(values, "cp", axis=0, tiled=True)
    count = key_piece.shape[0]
    key_heads = key_piece.reshape(count, H, HD)
    value_heads = value_piece.astype(jnp.float32).reshape(count, H, HD)
    allowed = allowed_mask(count)
    scores = (
        jnp.einsum("qhd,khd->hqk", query_heads, key_heads, preferred_element_type=jnp.float32)
        * scale
    )
    scores = jnp.where(allowed, scores, -1e30)
    new_top = jnp.maximum(running_top, jnp.max(scores, axis=-1))
    factor = jnp.exp(running_top - new_top)
    probs = jnp.where(allowed, jnp.exp(scores - new_top[..., None]), 0.0)
    running_total = jnp.sum(probs, axis=-1)
    update = jnp.einsum("hqk,khd->qhd", probs, value_heads, precision=lax.Precision.HIGHEST)
    weighted = weighted * factor.T[..., None] + update
    weighted, running_top, running_total = (weighted, new_top, running_total)
    out_exact = weighted / running_total.T[..., None]
    logsum = running_top + jnp.log(running_total)
    attended_low = out_exact.reshape(token_rows, D).astype(jnp.bfloat16)
    middle = inputs + (
        jnp.dot(attended_low, out_full, preferred_element_type=jnp.float32)
        + out_bias.astype(jnp.float32)
    )
    normed_two, norm_two_back = jax.vjp(
        layer_norm, middle, gain_two.astype(jnp.float32), shift_two.astype(jnp.float32)
    )
    normed_two_low = normed_two.astype(jnp.bfloat16)
    hidden = jnp.dot(normed_two_low, in_full, preferred_element_type=jnp.float32) + in_bias.astype(
        jnp.float32
    )
    active, gelu_back = jax.vjp(partial(jax.nn.gelu, approximate=True), hidden)
    active_low = active.astype(jnp.bfloat16)
    result = (
        middle
        + jnp.dot(active_low, down_full, preferred_element_type=jnp.float32)
        + down_bias.astype(jnp.float32)
    )
    layer_out = result.astype(jnp.bfloat16)
    qkv_back, out_back, in_back, down_back = (
        lax.all_gather(w_qkv, "cp", axis=0, tiled=True),
        lax.all_gather(w_out, "cp", axis=0, tiled=True),
        lax.all_gather(w_in, "cp", axis=0, tiled=True),
        lax.all_gather(w_down, "cp", axis=0, tiled=True),
    )
    grad_output = cotangent.astype(jnp.float32)
    grad_down = across_rows(active_low, cotangent)
    grad_down_bias = jnp.sum(grad_output, axis=0)
    grad_active = along_rows(cotangent, down_back)
    grad_hidden = gelu_back(grad_active)[0].astype(jnp.bfloat16)
    grad_in = across_rows(normed_two_low, grad_hidden)
    grad_in_bias = jnp.sum(grad_hidden.astype(jnp.float32), axis=0)
    grad_middle_part, grad_gain_two, grad_shift_two = norm_two_back(
        along_rows(grad_hidden, in_back)
    )
    grad_middle = grad_output + grad_middle_part
    grad_branch = grad_middle.astype(jnp.bfloat16)
    grad_out_proj = across_rows(attended_low, grad_branch)
    grad_out_bias = jnp.sum(grad_branch.astype(jnp.float32), axis=0)
    grad_attended = along_rows(grad_branch, out_back).astype(jnp.bfloat16)
    grad_heads = grad_attended.reshape(token_rows, H, HD)
    grad_heads_float = grad_heads.astype(jnp.float32)
    delta = jnp.einsum("qhd,qhd->hq", grad_heads_float, out_exact)
    key_piece = lax.all_gather(keys, "cp", axis=0, tiled=True)
    value_piece = lax.all_gather(values, "cp", axis=0, tiled=True)
    count = key_piece.shape[0]
    key_heads = key_piece.reshape(count, H, HD)
    value_heads = value_piece.reshape(count, H, HD)
    allowed = allowed_mask(count)
    scores = (
        jnp.einsum("qhd,khd->hqk", query_heads, key_heads, preferred_element_type=jnp.float32)
        * scale
    )
    probs = jnp.where(allowed, jnp.exp(scores - logsum[..., None]), 0.0)
    grad_probs = jnp.einsum(
        "qhd,khd->hqk", grad_heads, value_heads, preferred_element_type=jnp.float32
    )
    grad_scores = (probs * (grad_probs - delta[..., None])).astype(jnp.bfloat16)
    grad_query = jnp.einsum(
        "hqk,khd->qhd", grad_scores, key_heads, preferred_element_type=jnp.float32
    )
    paired = jnp.concatenate([keys, values], axis=1)
    piece = lax.all_gather(paired, "cp", axis=0, tiled=True)
    count = piece.shape[0]
    key_heads = piece[:, :D].reshape(count, H, HD)
    value_heads = piece[:, D:].reshape(count, H, HD)
    allowed = allowed_mask(count)
    scores = (
        jnp.einsum("qhd,khd->hqk", query_heads, key_heads, preferred_element_type=jnp.float32)
        * scale
    )
    probs = jnp.where(allowed, jnp.exp(scores - logsum[..., None]), 0.0)
    grad_probs = jnp.einsum(
        "qhd,khd->hqk", grad_heads, value_heads, preferred_element_type=jnp.float32
    )
    grad_scores = (probs * (grad_probs - delta[..., None])).astype(jnp.bfloat16)
    key_term = (
        jnp.einsum(
            "hqk,qhd->khd", grad_scores, query_heads, preferred_element_type=jnp.float32
        ).reshape(count, D)
        * scale
    )
    value_term = jnp.einsum(
        "hqk,qhd->khd", probs, grad_heads_float, precision=lax.Precision.HIGHEST
    ).reshape(count, D)
    terms = jnp.concatenate([key_term, value_term], axis=1)
    owned_terms = lax.psum_scatter(terms, "cp", scatter_dimension=0, tiled=True)
    grad_keys = owned_terms[:, :D]
    grad_values = owned_terms[:, D:]
    grad_query_low = (grad_query * scale).reshape(token_rows, D).astype(jnp.bfloat16)
    grad_mixed = jnp.concatenate(
        [grad_query_low, grad_keys.astype(jnp.bfloat16), grad_values.astype(jnp.bfloat16)], axis=1
    )
    grad_qkv = across_rows(normed_low, grad_mixed)
    mixed_sums = jnp.sum(grad_mixed.astype(jnp.float32), axis=0)
    grad_qv_bias = jnp.concatenate([mixed_sums[:D], mixed_sums[2 * D :]])
    grad_input_part, grad_gain_one, grad_shift_one = norm_one_back(along_rows(grad_mixed, qkv_back))
    input_grad = (grad_middle + grad_input_part).astype(jnp.bfloat16)
    owned = (
        lax.psum_scatter(grad_gain_one, "cp", scatter_dimension=0, tiled=True),
        lax.psum_scatter(grad_shift_one, "cp", scatter_dimension=0, tiled=True),
        lax.psum_scatter(grad_qkv, "cp", scatter_dimension=0, tiled=True),
        lax.psum_scatter(grad_qv_bias, "cp", scatter_dimension=0, tiled=True),
        lax.psum_scatter(grad_out_proj, "cp", scatter_dimension=0, tiled=True),
        lax.psum_scatter(grad_out_bias, "cp", scatter_dimension=0, tiled=True),
        lax.psum_scatter(grad_gain_two, "cp", scatter_dimension=0, tiled=True),
        lax.psum_scatter(grad_shift_two, "cp", scatter_dimension=0, tiled=True),
        lax.psum_scatter(grad_in, "cp", scatter_dimension=0, tiled=True),
        lax.psum_scatter(grad_in_bias, "cp", scatter_dimension=0, tiled=True),
        lax.psum_scatter(grad_down, "cp", scatter_dimension=0, tiled=True),
        lax.psum_scatter(grad_down_bias, "cp", scatter_dimension=0, tiled=True),
    )
    totals = lax.psum(
        (
            owned[0],
            owned[1],
            owned[2],
            owned[3],
            owned[4],
            owned[5],
            owned[6],
            owned[7],
            owned[8],
            owned[9],
            owned[10],
            owned[11],
        ),
        "rep",
    )
    return (layer_out, input_grad) + tuple(totals)


BF = jnp.bfloat16
F32 = jnp.float32
MESH = pl.DeviceIdType.MESH
VM = pl.BlockSpec(memory_space=pltpu.VMEM)
CHUNKS = 4


def params(collective_id=None, **more):
    if collective_id is not None:
        more.update(collective_id=collective_id, has_side_effects=True)
    return pltpu.CompilerParams(vmem_limit_bytes=48 * 2**20, **more)


def places():
    me = lax.axis_index("cp")
    core = lax.rem(me, 2)
    row = me // 2
    return me, row * 2 + 1 - core, (1 - row) * 2 + core, (1 - row) * 2 + 1 - core


def greet(*others):
    barrier = pltpu.get_barrier_semaphore()
    for other in others:
        pl.semaphore_signal(barrier, inc=1, device_id={"cp": other}, device_id_type=MESH)
    pl.semaphore_wait(barrier, len(others))


def push(src, dst, send, recv, other):
    return pltpu.make_async_remote_copy(
        src_ref=src, dst_ref=dst, send_sem=send, recv_sem=recv,
        device_id={"cp": other}, device_id_type=MESH,
    )


def open_kernel(x_ref, w_ref, s_ref, xa_ref, wa_ref, sa_ref, send, recv):
    me, sib, opp, diag = places()
    greet(sib, opp, diag)
    part = x_ref.shape[0] // CHUNKS
    pieces = [pl.ds(k * part, part) for k in range(CHUNKS)]
    across = [
        push(x_ref.at[p], xa_ref.at[me, p], send.at[k], recv.at[k], opp)
        for k, p in enumerate(pieces)
    ]
    slot = CHUNKS
    rest = []
    for other in (opp, diag, sib):
        rest.append(push(s_ref, sa_ref.at[me], send.at[slot], recv.at[slot], other))
        rest.append(push(w_ref.at[other], wa_ref.at[me], send.at[slot + 1], recv.at[slot + 1], other))
        slot += 2
    rest.append(push(x_ref, xa_ref.at[me], send.at[slot], recv.at[slot], sib))
    slot += 1
    for copy in across + rest:
        copy.start()
    xa_ref[me] = x_ref[...]
    wa_ref[me] = w_ref[me]
    sa_ref[me] = s_ref[...]
    onward = []
    for k, p in enumerate(pieces):
        across[k].wait_recv()
        copy = push(xa_ref.at[opp, p], xa_ref.at[opp, p], send.at[slot + k], recv.at[slot + k], sib)
        copy.start()
        onward.append(copy)
    for copy in across:
        copy.wait_send()
    for copy in rest + onward:
        copy.wait()


def open_exchange(x, w, s):
    n = w.shape[0]
    count = 2 * CHUNKS + 7
    return pl.pallas_call(
        open_kernel,
        out_shape=[
            jax.ShapeDtypeStruct((n,) + x.shape, x.dtype),
            jax.ShapeDtypeStruct(w.shape, w.dtype),
            jax.ShapeDtypeStruct((n,) + s.shape, s.dtype),
        ],
        in_specs=[VM] * 3,
        out_specs=[VM] * 3,
        scratch_shapes=[pltpu.SemaphoreType.DMA((count,))] * 2,
        compiler_params=params(0),
        name="open_exchange",
    )(x, w, s)


def swap_kernel(w_ref, wa_ref, send, recv):
    me, sib, opp, diag = places()
    greet(sib, opp, diag)
    copies = []
    for k, other in enumerate((opp, diag, sib)):
        copies.append(push(w_ref.at[other], wa_ref.at[me], send.at[k], recv.at[k], other))
        copies[-1].start()
    wa_ref[me] = w_ref[me]
    for copy in copies:
        copy.wait()


def swap(w, collective_id):
    return pl.pallas_call(
        swap_kernel,
        out_shape=jax.ShapeDtypeStruct(w.shape, w.dtype),
        in_specs=[VM],
        out_specs=VM,
        scratch_shapes=[pltpu.SemaphoreType.DMA((3,))] * 2,
        compiler_params=params(collective_id),
        name="swap",
    )(w)


class Reduce:
    def __init__(self, p_ref, near, sent, far, send, recv):
        self.me, self.sib, self.opp, self.diag = places()
        self.refs = (p_ref, near, sent, far)
        self.part = part = p_ref.shape[1] // CHUNKS
        self.pieces = [pl.ds(k * part, part) for k in range(CHUNKS)]
        self.first, self.own, self.across = [], [], []
        for k, p in enumerate(self.pieces):
            self.first.append(push(p_ref.at[self.diag, p], near.at[0, p], send.at[k], recv.at[k], self.sib))
            self.own.append(push(p_ref.at[self.sib, p], near.at[1, p], send.at[CHUNKS + k], recv.at[CHUNKS + k], self.sib))
            self.across.append(push(sent.at[p], far.at[p], send.at[2 * CHUNKS + k], recv.at[2 * CHUNKS + k], self.opp))

    def start(self):
        p_ref, near, sent, far = self.refs
        for copy in self.first + self.own:
            copy.start()
        for k, p in enumerate(self.pieces):
            self.first[k].wait_recv()
            sent[p] = (p_ref[self.opp, p].astype(F32) + near[0, p].astype(F32)).astype(BF)
            self.across[k].start()

    def piece(self, k):
        p_ref, near, sent, far = self.refs
        p = self.pieces[k]
        self.own[k].wait_recv()
        self.across[k].wait_recv()
        return p_ref[self.me, p].astype(F32) + near[1, p].astype(F32) + far[p].astype(F32)

    def finish(self):
        for copy in self.first + self.own + self.across:
            copy.wait_send()


class Gather:
    def __init__(self, x_ref, all_ref, send, recv, base):
        self.me, self.sib, self.opp, self.diag = places()
        part = x_ref.shape[0] // CHUNKS
        self.pieces = [pl.ds(k * part, part) for k in range(CHUNKS)]
        self.across, self.near, self.onward = [], [], []
        me, sib, opp = self.me, self.sib, self.opp
        for k, p in enumerate(self.pieces):
            a, b, c = base + k, base + CHUNKS + k, base + 2 * CHUNKS + k
            self.across.append(push(x_ref.at[p], all_ref.at[me, p], send.at[a], recv.at[a], opp))
            self.near.append(push(x_ref.at[p], all_ref.at[me, p], send.at[b], recv.at[b], sib))
            self.onward.append(push(all_ref.at[opp, p], all_ref.at[opp, p], send.at[c], recv.at[c], sib))

    def start(self, k):
        self.across[k].start()
        self.near[k].start()

    def finish(self):
        for k in range(CHUNKS):
            self.across[k].wait_recv()
            self.onward[k].start()
        for copy in self.across:
            copy.wait_send()
        for copy in self.near + self.onward:
            copy.wait()


def normalise(values):
    centred = values - jnp.mean(values, axis=-1, keepdims=True)
    variance = jnp.mean(centred * centred, axis=-1, keepdims=True)
    scale = lax.rsqrt(variance + 1e-05)
    return centred * scale, scale


def norm_back(upstream, gain, unit, scale):
    inner = upstream * gain
    return scale * (
        inner
        - jnp.mean(inner, axis=-1, keepdims=True)
        - unit * jnp.mean(inner * unit, axis=-1, keepdims=True)
    )


def middle_kernel(p_ref, x_ref, vec_ref, r_ref, all_ref, near, sent, far, mine, send, recv):
    me, sib, opp, diag = places()
    greet(sib, opp)
    reduce = Reduce(p_ref, near, sent, far, send, recv)
    gather = Gather(mine, all_ref, send, recv, 3 * CHUNKS)
    reduce.start()
    for k, p in enumerate(reduce.pieces):
        r = x_ref[p].astype(F32) + (reduce.piece(k) + vec_ref[0:1])
        r_ref[p] = r
        unit, _ = normalise(r)
        low = (unit * vec_ref[1:2] + vec_ref[2:3]).astype(BF)
        mine[p] = low
        gather.start(k)
        all_ref[me, p] = low
    gather.finish()
    reduce.finish()


def reduce_scratch(rows, wide):
    return [
        pltpu.VMEM((2, rows, wide), BF),
        pltpu.VMEM((rows, wide), BF),
        pltpu.VMEM((rows, wide), BF),
    ]


def middle_step(p, x, vec):
    n, rows, wide = p.shape
    return pl.pallas_call(
        middle_kernel,
        out_shape=[
            jax.ShapeDtypeStruct((rows, wide), F32),
            jax.ShapeDtypeStruct((n, rows, wide), BF),
        ],
        in_specs=[VM] * 3,
        out_specs=[VM] * 2,
        scratch_shapes=reduce_scratch(rows, wide)
        + [pltpu.VMEM((rows, wide), BF)]
        + [pltpu.SemaphoreType.DMA((6 * CHUNKS,))] * 2,
        compiler_params=params(1),
        name="middle_step",
    )(p, x, vec)


def back_kernel(p_ref, r_ref, g_ref, vec_ref, gr_ref, all_ref, sums_ref, near, sent, far, mine, send, recv):
    me, sib, opp, diag = places()
    greet(sib, opp)
    reduce = Reduce(p_ref, near, sent, far, send, recv)
    gather = Gather(mine, all_ref, send, recv, 3 * CHUNKS)
    reduce.start()
    sums_ref[...] = jnp.zeros_like(sums_ref)
    for k, p in enumerate(reduce.pieces):
        unit, scale = normalise(r_ref[p])
        g = g_ref[p].astype(F32)
        upstream = reduce.piece(k)
        gr = g + norm_back(upstream, vec_ref[1:2], unit, scale)
        gr_ref[p] = gr
        low = gr.astype(BF)
        mine[p] = low
        gather.start(k)
        all_ref[me, p] = low
        sums_ref[0:1] += jnp.sum(upstream * unit, axis=0, keepdims=True)
        sums_ref[1:2] += jnp.sum(upstream, axis=0, keepdims=True)
        sums_ref[2:3] += jnp.sum(low.astype(F32), axis=0, keepdims=True)
        sums_ref[3:4] += jnp.sum(g, axis=0, keepdims=True)
    gather.finish()
    reduce.finish()


def back_step(p, r, g, vec):
    n, rows, wide = p.shape
    return pl.pallas_call(
        back_kernel,
        out_shape=[
            jax.ShapeDtypeStruct((rows, wide), F32),
            jax.ShapeDtypeStruct((n, rows, wide), BF),
            jax.ShapeDtypeStruct((8, wide), F32),
        ],
        in_specs=[VM] * 4,
        out_specs=[VM] * 3,
        scratch_shapes=reduce_scratch(rows, wide)
        + [pltpu.VMEM((rows, wide), BF)]
        + [pltpu.SemaphoreType.DMA((6 * CHUNKS,))] * 2,
        compiler_params=params(2),
        name="back_step",
    )(p, r, g, vec)


def last_kernel(p_ref, x_ref, gr_ref, vec_ref, out_ref, sums_ref, near, sent, far, send, recv):
    me, sib, opp, diag = places()
    greet(sib, opp)
    reduce = Reduce(p_ref, near, sent, far, send, recv)
    reduce.start()
    sums_ref[...] = jnp.zeros_like(sums_ref)
    for k, p in enumerate(reduce.pieces):
        unit, scale = normalise(x_ref[p].astype(F32))
        upstream = reduce.piece(k)
        out_ref[p] = (gr_ref[p] + norm_back(upstream, vec_ref[0:1], unit, scale)).astype(BF)
        sums_ref[0:1] += jnp.sum(upstream * unit, axis=0, keepdims=True)
        sums_ref[1:2] += jnp.sum(upstream, axis=0, keepdims=True)
    reduce.finish()


def last_step(p, x, gr, vec):
    n, rows, wide = p.shape
    return pl.pallas_call(
        last_kernel,
        out_shape=[
            jax.ShapeDtypeStruct((rows, wide), BF),
            jax.ShapeDtypeStruct((8, wide), F32),
        ],
        in_specs=[VM] * 4,
        out_specs=[VM] * 2,
        scratch_shapes=reduce_scratch(rows, wide)
        + [pltpu.SemaphoreType.DMA((3 * CHUNKS,))] * 2,
        compiler_params=params(3),
        name="last_step",
    )(p, x, gr, vec)


def head_mask(wide):
    lane = lax.broadcasted_iota(jnp.int32, (1, wide), 1)
    low = pl.program_id(0) * HD
    return (lane >= low) & (lane < low + HD)


def causal(block, first, count):
    row = lax.broadcasted_iota(jnp.int32, (block, count), 0) + first
    return row >= lax.broadcasted_iota(jnp.int32, (block, count), 1)


def attend_kernel(block, q_ref, k_ref, v_ref, o_ref, lse_ref):
    length, wide = q_ref.shape
    mask = head_mask(wide)
    for first in range(0, length, block):
        count = first + block
        rows = slice(first, count)
        q = jnp.where(mask, q_ref[rows], 0) * BF(HD**-0.5)
        s = jnp.where(causal(block, first, count), along_rows(q, k_ref[:count]), -1e30)
        top = jnp.max(s, axis=-1, keepdims=True)
        p = jnp.exp(s - top)
        total = jnp.sum(p, axis=-1, keepdims=True)
        o = jnp.dot(p.astype(BF), v_ref[:count], preferred_element_type=F32) / total
        o_ref[rows] = jnp.where(mask, o.astype(BF), o_ref[rows])
        lse_ref[0, rows] = jnp.broadcast_to(top + jnp.log(total), (block, 128))


def attend(q, k, v):
    length, wide = q.shape
    heads = wide // HD
    whole = pl.BlockSpec((length, wide), lambda h: (0, 0))
    return pl.pallas_call(
        partial(attend_kernel, min(256, length)),
        grid=(heads,),
        out_shape=[
            jax.ShapeDtypeStruct((length, wide), BF),
            jax.ShapeDtypeStruct((heads, length, 128), F32),
        ],
        in_specs=[whole] * 3,
        out_specs=[whole, pl.BlockSpec((1, length, 128), lambda h: (h, 0, 0))],
        compiler_params=params(),
        cost_estimate=pl.CostEstimate(flops=4 * heads * length * length * 256, bytes_accessed=8 * length * wide, transcendentals=heads * length * length),
        name="attend",
    )(q, k, v)


def attend_back_kernel(block, q_ref, k_ref, v_ref, go_ref, lse_ref, gq_ref, gk_ref, gv_ref, gk_sum, gv_sum):
    length, wide = q_ref.shape
    mask = head_mask(wide)

    @pl.when(pl.program_id(0) == 0)
    def _():
        gk_sum[...] = jnp.zeros_like(gk_sum)
        gv_sum[...] = jnp.zeros_like(gv_sum)

    for first in range(0, length, block):
        count = first + block
        rows = slice(first, count)
        q = jnp.where(mask, q_ref[rows], 0) * BF(HD**-0.5)
        go = jnp.where(mask, go_ref[rows], 0)
        s = along_rows(q, k_ref[:count])
        p = jnp.where(causal(block, first, count), jnp.exp(s - lse_ref[0, rows, 0:1]), 0.0)
        dp = along_rows(go, v_ref[:count])
        delta = jnp.sum(p * dp, axis=-1, keepdims=True)
        ds = (p * (dp - delta)).astype(BF)
        gq = jnp.dot(ds, k_ref[:count], preferred_element_type=F32) * HD**-0.5
        gq_ref[rows] = jnp.where(mask, gq.astype(BF), gq_ref[rows])
        gk_sum[:count] += across_rows(ds, q)
        gv_sum[:count] += across_rows(p.astype(BF), go)

    @pl.when(pl.program_id(0) == pl.num_programs(0) - 1)
    def _():
        gk_ref[...] = gk_sum[...].astype(BF)
        gv_ref[...] = gv_sum[...].astype(BF)


def attend_back(q, k, v, go, lse):
    length, wide = q.shape
    heads = wide // HD
    whole = pl.BlockSpec((length, wide), lambda h: (0, 0))
    return pl.pallas_call(
        partial(attend_back_kernel, min(256, length)),
        grid=(heads,),
        out_shape=[jax.ShapeDtypeStruct((length, wide), BF)] * 3,
        in_specs=[whole] * 4 + [pl.BlockSpec((1, length, 128), lambda h: (h, 0, 0))],
        out_specs=[whole] * 3,
        scratch_shapes=[pltpu.VMEM((length, wide), F32)] * 2,
        compiler_params=params(),
        cost_estimate=pl.CostEstimate(flops=10 * heads * length * length * 256, bytes_accessed=16 * length * wide, transcendentals=heads * length * length),
        name="attend_back",
    )(q, k, v, go, lse)


def turn(blocks, n):
    me = lax.axis_index("cp")
    result = jnp.zeros_like(blocks)
    result = lax.dynamic_update_index_in_dim(result, lax.dynamic_index_in_dim(blocks, me, 0), me, 0)
    for step in range(1, n):
        there, back = lax.rem(me + step, n), lax.rem(me + n - step, n)
        got = lax.ppermute(
            lax.dynamic_index_in_dim(blocks, there, 0), "cp", [(i, (i + step) % n) for i in range(n)]
        )
        result = lax.dynamic_update_index_in_dim(result, got, back, 0)
    return result


def head_body(
    tokens, cotangent, ln1_gain, ln1_bias, w_qkv, b_qv, w_out, b_out,
    ln2_gain, ln2_bias, w_in, b_in, w_down, b_down, *, n,
):
    rows = tokens.shape[0]
    length = rows * n
    me = lax.axis_index("cp")
    share = D // n
    ff_share = w_in.shape[1] // n
    tidy = jnp.concatenate([ln1_gain, ln1_bias, b_out, ln2_gain, ln2_bias, b_down, b_qv])
    tidy = jnp.concatenate([tidy, jnp.zeros((-tidy.shape[0] % 2048,), BF)]).reshape(-1, 128)
    w_blocks = w_qkv.reshape(share, 3, n, share).transpose(2, 0, 1, 3).reshape(n, share, 3 * share)
    x_all, w_mine, tidy_all = open_exchange(tokens, w_blocks, tidy)
    x_all, late_in, late_cot = lax.optimization_barrier((x_all, w_in, cotangent))
    in_cols = turn(late_in.reshape(share, n, ff_share).transpose(1, 0, 2), n).reshape(D, ff_share)
    cot_all = lax.all_gather(late_cot, "cp", axis=0, tiled=True)
    w_mine = w_mine.reshape(D, 3 * share)
    tidy_all = tidy_all.reshape(n, -1).astype(F32)
    gain_one, shift_one, out_bias, gain_two, shift_two, down_bias = (
        tidy_all[:, i * share : (i + 1) * share].reshape(D) for i in range(6)
    )
    qv_bias = tidy_all[:, 6 * share : 8 * share].reshape(2, D)
    qv_mine = lax.dynamic_slice_in_dim(qv_bias, me * share, share, 1)
    vec_two = jnp.concatenate([jnp.stack([out_bias, gain_two, shift_two]), jnp.zeros((5, D), F32)])
    vec_one = jnp.concatenate([gain_one[None], jnp.zeros((7, D), F32)])

    n1 = layer_norm(x_all.reshape(length, D).astype(F32), gain_one, shift_one).astype(BF)
    mixed = jnp.dot(n1, w_mine, preferred_element_type=F32)
    q = (mixed[:, :share] + qv_mine[0]).astype(BF)
    k = mixed[:, share : 2 * share].astype(BF)
    v = (mixed[:, 2 * share :] + qv_mine[1]).astype(BF)
    o, lse = attend(q, k, v)
    o_part = jnp.dot(o, w_out, preferred_element_type=F32).astype(BF).reshape(n, rows, D)
    r, n2 = middle_step(o_part, tokens, vec_two)
    n2 = n2.reshape(length, D)
    hidden = jnp.dot(n2, in_cols, preferred_element_type=F32) + b_in.astype(F32)
    active, gelu_back = jax.vjp(partial(jax.nn.gelu, approximate=True), hidden)
    a = active.astype(BF)
    y_part = jnp.dot(a, w_down, preferred_element_type=F32).astype(BF)
    gu = gelu_back(along_rows(cot_all, w_down))[0].astype(BF)
    n2_part = along_rows(gu, in_cols).astype(BF).reshape(n, rows, D)
    grad_down = across_rows(a, cot_all).astype(BF)
    grad_in = across_rows(n2, gu).astype(BF).reshape(n, share, ff_share)
    grad_in_bias = jnp.sum(gu.astype(F32), axis=0)
    grad_down = lax.psum(grad_down, "rep")

    gr, gz, sums_two = back_step(n2_part, r, cotangent, vec_two)
    gz, y_part, grad_in = lax.optimization_barrier((gz, y_part, grad_in))
    y = lax.psum_scatter(y_part, "cp", scatter_dimension=0, tiled=True)
    layer_out = (r + y.astype(F32) + down_bias).astype(BF)
    grad_in = turn(grad_in, n).transpose(1, 0, 2).reshape(share, n * ff_share)
    gz = gz.reshape(length, D)
    go = along_rows(gz, w_out).astype(BF)
    grad_out = across_rows(o, gz).astype(BF)
    grad_out, grad_in, grad_down = lax.optimization_barrier((grad_out, grad_in, grad_down))
    grad_out, grad_in = lax.psum((grad_out, grad_in), "rep")
    gq, gk, gv = attend_back(q, k, v, go, lse)
    gm = jnp.concatenate([gq, gk, gv], axis=1)
    grad_qkv = swap(across_rows(n1, gm).astype(BF).reshape(n, share, 3 * share), 4)
    grad_qkv = grad_qkv.reshape(n, share, 3, share).transpose(1, 2, 0, 3).reshape(share, 3 * D)
    grad_qkv, grad_out, grad_in = lax.optimization_barrier((grad_qkv, grad_out, grad_in))
    grad_qkv = lax.psum(grad_qkv, "rep").astype(F32)
    grad_out, grad_in, grad_down = grad_out.astype(F32), grad_in.astype(F32), grad_down.astype(F32)
    n1_part = along_rows(gm, w_mine).astype(BF).reshape(n, rows, D)
    input_grad, sums_one = last_step(n1_part, tokens, gr, vec_one)

    qv_sums = jnp.zeros((2, D), F32)
    qv_sums = lax.dynamic_update_slice(
        qv_sums,
        jnp.stack([jnp.sum(gq.astype(F32), axis=0), jnp.sum(gv.astype(F32), axis=0)]),
        (0, me * share),
    )
    in_sums = lax.dynamic_update_slice(jnp.zeros((n * ff_share,), F32), grad_in_bias, (me * ff_share,))
    sums = lax.psum(
        jnp.concatenate([sums_one[:2], sums_two[:4], qv_sums, in_sums.reshape(-1, D)]), ("rep", "cp")
    )
    own = lax.dynamic_slice_in_dim(sums[:6], me * share, share, 1)
    own_qv = lax.dynamic_slice_in_dim(sums[6:8].reshape(-1), me * 2 * share, 2 * share, 0)
    own_in = lax.dynamic_slice_in_dim(sums[8:].reshape(-1), me * ff_share, ff_share, 0)
    return (
        layer_out, input_grad, own[0], own[1], grad_qkv, own_qv, grad_out, own[4],
        own[2], own[3], grad_in, own_in, grad_down, own[5],
    )


def solution(mesh):
    placed = (
        P(("rep", "cp"), None),
        P(("rep", "cp"), None),
        P("cp"),
        P("cp"),
        P("cp", None),
        P("cp"),
        P("cp", None),
        P("cp"),
        P("cp"),
        P("cp"),
        P("cp", None),
        P("cp"),
        P("cp", None),
        P("cp"),
    )
    count = mesh.shape["cp"]
    by_heads = count == 4 and H % count == 0
    return jax.shard_map(
        partial(head_body, n=count) if by_heads else body,
        mesh=mesh,
        in_specs=placed,
        out_specs=(
            P(("rep", "cp"), None),
            P(("rep", "cp"), None),
            P("cp"),
            P("cp"),
            P("cp", None),
            P("cp"),
            P("cp", None),
            P("cp"),
            P("cp"),
            P("cp"),
            P("cp", None),
            P("cp"),
            P("cp", None),
            P("cp"),
        ),
        check_vma=False,
    )
```

```python
from functools import partial

import jax
import jax.numpy as jnp
from jax import lax
from jax.experimental import pallas as pl
from jax.experimental.pallas import tpu as pltpu
from jax.sharding import PartitionSpec as P

D = 768
H = 12
HD = 64


def layer_norm(values, gain, shift):
    centred = values - jnp.mean(values, axis=-1, keepdims=True)
    variance = jnp.mean(centred * centred, axis=-1, keepdims=True)
    return centred * lax.rsqrt(variance + 1e-05) * gain + shift


def along_rows(left, right):
    return lax.dot_general(
        left, right, (((1,), (1,)), ((), ())), preferred_element_type=jnp.float32
    )


def across_rows(left, right):
    return lax.dot_general(
        left, right, (((0,), (0,)), ((), ())), preferred_element_type=jnp.float32
    )


def body(
    tokens,
    cotangent,
    ln1_gain,
    ln1_bias,
    w_qkv,
    b_qv,
    w_out,
    b_out,
    ln2_gain,
    ln2_bias,
    w_in,
    b_in,
    w_down,
    b_down,
):
    (
        gain_one,
        shift_one,
        qkv_full,
        qv_bias,
        out_full,
        out_bias,
        gain_two,
        shift_two,
        in_full,
        in_bias,
        down_full,
        down_bias,
    ) = (
        lax.all_gather(ln1_gain, "cp", axis=0, tiled=True),
        lax.all_gather(ln1_bias, "cp", axis=0, tiled=True),
        lax.all_gather(w_qkv, "cp", axis=0, tiled=True),
        lax.all_gather(b_qv, "cp", axis=0, tiled=True),
        lax.all_gather(w_out, "cp", axis=0, tiled=True),
        lax.all_gather(b_out, "cp", axis=0, tiled=True),
        lax.all_gather(ln2_gain, "cp", axis=0, tiled=True),
        lax.all_gather(ln2_bias, "cp", axis=0, tiled=True),
        lax.all_gather(w_in, "cp", axis=0, tiled=True),
        lax.all_gather(b_in, "cp", axis=0, tiled=True),
        lax.all_gather(w_down, "cp", axis=0, tiled=True),
        lax.all_gather(b_down, "cp", axis=0, tiled=True),
    )
    token_rows = tokens.shape[0]
    first_row = lax.axis_index("cp") * token_rows
    scale = HD ** (-0.5)
    query_places = first_row + jnp.arange(token_rows, dtype=jnp.int32)

    def allowed_mask(count):
        return (query_places[:, None] >= jnp.arange(count, dtype=jnp.int32)[None, :])[None]

    inputs = tokens.astype(jnp.float32)
    normed, norm_one_back = jax.vjp(
        layer_norm, inputs, gain_one.astype(jnp.float32), shift_one.astype(jnp.float32)
    )
    normed_low = normed.astype(jnp.bfloat16)
    mixed = jnp.dot(normed_low, qkv_full, preferred_element_type=jnp.float32)
    bias_float = qv_bias.astype(jnp.float32)
    query = (mixed[:, :D] + bias_float[:D]).astype(jnp.bfloat16)
    keys = mixed[:, D : 2 * D].astype(jnp.bfloat16)
    values = (mixed[:, 2 * D :] + bias_float[D:]).astype(jnp.bfloat16)
    query_heads = query.reshape(token_rows, H, HD)
    weighted = jnp.zeros((token_rows, H, HD), jnp.float32)
    running_top = jnp.full((H, token_rows), -1e30, jnp.float32)
    key_piece = lax.all_gather(keys, "cp", axis=0, tiled=True)
    value_piece = lax.all_gather(values, "cp", axis=0, tiled=True)
    count = key_piece.shape[0]
    key_heads = key_piece.reshape(count, H, HD)
    value_heads = value_piece.astype(jnp.float32).reshape(count, H, HD)
    allowed = allowed_mask(count)
    scores = (
        jnp.einsum("qhd,khd->hqk", query_heads, key_heads, preferred_element_type=jnp.float32)
        * scale
    )
    scores = jnp.where(allowed, scores, -1e30)
    new_top = jnp.maximum(running_top, jnp.max(scores, axis=-1))
    factor = jnp.exp(running_top - new_top)
    probs = jnp.where(allowed, jnp.exp(scores - new_top[..., None]), 0.0)
    running_total = jnp.sum(probs, axis=-1)
    update = jnp.einsum("hqk,khd->qhd", probs, value_heads, precision=lax.Precision.HIGHEST)
    weighted = weighted * factor.T[..., None] + update
    weighted, running_top, running_total = (weighted, new_top, running_total)
    out_exact = weighted / running_total.T[..., None]
    logsum = running_top + jnp.log(running_total)
    attended_low = out_exact.reshape(token_rows, D).astype(jnp.bfloat16)
    middle = inputs + (
        jnp.dot(attended_low, out_full, preferred_element_type=jnp.float32)
        + out_bias.astype(jnp.float32)
    )
    normed_two, norm_two_back = jax.vjp(
        layer_norm, middle, gain_two.astype(jnp.float32), shift_two.astype(jnp.float32)
    )
    normed_two_low = normed_two.astype(jnp.bfloat16)
    hidden = jnp.dot(normed_two_low, in_full, preferred_element_type=jnp.float32) + in_bias.astype(
        jnp.float32
    )
    active, gelu_back = jax.vjp(partial(jax.nn.gelu, approximate=True), hidden)
    active_low = active.astype(jnp.bfloat16)
    result = (
        middle
        + jnp.dot(active_low, down_full, preferred_element_type=jnp.float32)
        + down_bias.astype(jnp.float32)
    )
    layer_out = result.astype(jnp.bfloat16)
    qkv_back, out_back, in_back, down_back = (
        lax.all_gather(w_qkv, "cp", axis=0, tiled=True),
        lax.all_gather(w_out, "cp", axis=0, tiled=True),
        lax.all_gather(w_in, "cp", axis=0, tiled=True),
        lax.all_gather(w_down, "cp", axis=0, tiled=True),
    )
    grad_output = cotangent.astype(jnp.float32)
    grad_down = across_rows(active_low, cotangent)
    grad_down_bias = jnp.sum(grad_output, axis=0)
    grad_active = along_rows(cotangent, down_back)
    grad_hidden = gelu_back(grad_active)[0].astype(jnp.bfloat16)
    grad_in = across_rows(normed_two_low, grad_hidden)
    grad_in_bias = jnp.sum(grad_hidden.astype(jnp.float32), axis=0)
    grad_middle_part, grad_gain_two, grad_shift_two = norm_two_back(
        along_rows(grad_hidden, in_back)
    )
    grad_middle = grad_output + grad_middle_part
    grad_branch = grad_middle.astype(jnp.bfloat16)
    grad_out_proj = across_rows(attended_low, grad_branch)
    grad_out_bias = jnp.sum(grad_branch.astype(jnp.float32), axis=0)
    grad_attended = along_rows(grad_branch, out_back).astype(jnp.bfloat16)
    grad_heads = grad_attended.reshape(token_rows, H, HD)
    grad_heads_float = grad_heads.astype(jnp.float32)
    delta = jnp.einsum("qhd,qhd->hq", grad_heads_float, out_exact)
    key_piece = lax.all_gather(keys, "cp", axis=0, tiled=True)
    value_piece = lax.all_gather(values, "cp", axis=0, tiled=True)
    count = key_piece.shape[0]
    key_heads = key_piece.reshape(count, H, HD)
    value_heads = value_piece.reshape(count, H, HD)
    allowed = allowed_mask(count)
    scores = (
        jnp.einsum("qhd,khd->hqk", query_heads, key_heads, preferred_element_type=jnp.float32)
        * scale
    )
    probs = jnp.where(allowed, jnp.exp(scores - logsum[..., None]), 0.0)
    grad_probs = jnp.einsum(
        "qhd,khd->hqk", grad_heads, value_heads, preferred_element_type=jnp.float32
    )
    grad_scores = (probs * (grad_probs - delta[..., None])).astype(jnp.bfloat16)
    grad_query = jnp.einsum(
        "hqk,khd->qhd", grad_scores, key_heads, preferred_element_type=jnp.float32
    )
    paired = jnp.concatenate([keys, values], axis=1)
    piece = lax.all_gather(paired, "cp", axis=0, tiled=True)
    count = piece.shape[0]
    key_heads = piece[:, :D].reshape(count, H, HD)
    value_heads = piece[:, D:].reshape(count, H, HD)
    allowed = allowed_mask(count)
    scores = (
        jnp.einsum("qhd,khd->hqk", query_heads, key_heads, preferred_element_type=jnp.float32)
        * scale
    )
    probs = jnp.where(allowed, jnp.exp(scores - logsum[..., None]), 0.0)
    grad_probs = jnp.einsum(
        "qhd,khd->hqk", grad_heads, value_heads, preferred_element_type=jnp.float32
    )
    grad_scores = (probs * (grad_probs - delta[..., None])).astype(jnp.bfloat16)
    key_term = (
        jnp.einsum(
            "hqk,qhd->khd", grad_scores, query_heads, preferred_element_type=jnp.float32
        ).reshape(count, D)
        * scale
    )
    value_term = jnp.einsum(
        "hqk,qhd->khd", probs, grad_heads_float, precision=lax.Precision.HIGHEST
    ).reshape(count, D)
    terms = jnp.concatenate([key_term, value_term], axis=1)
    owned_terms = lax.psum_scatter(terms, "cp", scatter_dimension=0, tiled=True)
    grad_keys = owned_terms[:, :D]
    grad_values = owned_terms[:, D:]
    grad_query_low = (grad_query * scale).reshape(token_rows, D).astype(jnp.bfloat16)
    grad_mixed = jnp.concatenate(
        [grad_query_low, grad_keys.astype(jnp.bfloat16), grad_values.astype(jnp.bfloat16)], axis=1
    )
    grad_qkv = across_rows(normed_low, grad_mixed)
    mixed_sums = jnp.sum(grad_mixed.astype(jnp.float32), axis=0)
    grad_qv_bias = jnp.concatenate([mixed_sums[:D], mixed_sums[2 * D :]])
    grad_input_part, grad_gain_one, grad_shift_one = norm_one_back(along_rows(grad_mixed, qkv_back))
    input_grad = (grad_middle + grad_input_part).astype(jnp.bfloat16)
    owned = (
        lax.psum_scatter(grad_gain_one, "cp", scatter_dimension=0, tiled=True),
        lax.psum_scatter(grad_shift_one, "cp", scatter_dimension=0, tiled=True),
        lax.psum_scatter(grad_qkv, "cp", scatter_dimension=0, tiled=True),
        lax.psum_scatter(grad_qv_bias, "cp", scatter_dimension=0, tiled=True),
        lax.psum_scatter(grad_out_proj, "cp", scatter_dimension=0, tiled=True),
        lax.psum_scatter(grad_out_bias, "cp", scatter_dimension=0, tiled=True),
        lax.psum_scatter(grad_gain_two, "cp", scatter_dimension=0, tiled=True),
        lax.psum_scatter(grad_shift_two, "cp", scatter_dimension=0, tiled=True),
        lax.psum_scatter(grad_in, "cp", scatter_dimension=0, tiled=True),
        lax.psum_scatter(grad_in_bias, "cp", scatter_dimension=0, tiled=True),
        lax.psum_scatter(grad_down, "cp", scatter_dimension=0, tiled=True),
        lax.psum_scatter(grad_down_bias, "cp", scatter_dimension=0, tiled=True),
    )
    totals = lax.psum(
        (
            owned[0],
            owned[1],
            owned[2],
            owned[3],
            owned[4],
            owned[5],
            owned[6],
            owned[7],
            owned[8],
            owned[9],
            owned[10],
            owned[11],
        ),
        "rep",
    )
    return (layer_out, input_grad) + tuple(totals)


BF = jnp.bfloat16
F32 = jnp.float32
MESH = pl.DeviceIdType.MESH
VM = pl.BlockSpec(memory_space=pltpu.VMEM)
CHUNKS = 4


def params(collective_id=None, **more):
    if collective_id is not None:
        more.update(collective_id=collective_id, has_side_effects=True)
    return pltpu.CompilerParams(vmem_limit_bytes=48 * 2**20, **more)


def places():
    me = lax.axis_index("cp")
    core = lax.rem(me, 2)
    row = me // 2
    return me, row * 2 + 1 - core, (1 - row) * 2 + core, (1 - row) * 2 + 1 - core


def greet(*others):
    barrier = pltpu.get_barrier_semaphore()
    for other in others:
        pl.semaphore_signal(barrier, inc=1, device_id={"cp": other}, device_id_type=MESH)
    pl.semaphore_wait(barrier, len(others))


def push(src, dst, send, recv, other):
    return pltpu.make_async_remote_copy(
        src_ref=src, dst_ref=dst, send_sem=send, recv_sem=recv,
        device_id={"cp": other}, device_id_type=MESH,
    )


def open_kernel(x_ref, w_ref, s_ref, xa_ref, wa_ref, sa_ref, send, recv):
    me, sib, opp, diag = places()
    greet(sib, opp, diag)
    part = x_ref.shape[0] // CHUNKS
    pieces = [pl.ds(k * part, part) for k in range(CHUNKS)]
    across = [
        push(x_ref.at[p], xa_ref.at[me, p], send.at[k], recv.at[k], opp)
        for k, p in enumerate(pieces)
    ]
    slot = CHUNKS
    rest = []
    for other in (opp, diag, sib):
        rest.append(push(s_ref, sa_ref.at[me], send.at[slot], recv.at[slot], other))
        rest.append(push(w_ref.at[other], wa_ref.at[me], send.at[slot + 1], recv.at[slot + 1], other))
        slot += 2
    rest.append(push(x_ref, xa_ref.at[me], send.at[slot], recv.at[slot], sib))
    slot += 1
    for copy in across + rest:
        copy.start()
    xa_ref[me] = x_ref[...]
    wa_ref[me] = w_ref[me]
    sa_ref[me] = s_ref[...]
    onward = []
    for k, p in enumerate(pieces):
        across[k].wait_recv()
        copy = push(xa_ref.at[opp, p], xa_ref.at[opp, p], send.at[slot + k], recv.at[slot + k], sib)
        copy.start()
        onward.append(copy)
    for copy in across:
        copy.wait_send()
    for copy in rest + onward:
        copy.wait()


def open_exchange(x, w, s):
    n = w.shape[0]
    count = 2 * CHUNKS + 7
    return pl.pallas_call(
        open_kernel,
        out_shape=[
            jax.ShapeDtypeStruct((n,) + x.shape, x.dtype),
            jax.ShapeDtypeStruct(w.shape, w.dtype),
            jax.ShapeDtypeStruct((n,) + s.shape, s.dtype),
        ],
        in_specs=[VM] * 3,
        out_specs=[VM] * 3,
        scratch_shapes=[pltpu.SemaphoreType.DMA((count,))] * 2,
        compiler_params=params(0),
        name="open_exchange",
    )(x, w, s)


def swap_kernel(w_ref, wa_ref, send, recv):
    me, sib, opp, diag = places()
    greet(sib, opp, diag)
    copies = []
    for k, other in enumerate((opp, diag, sib)):
        copies.append(push(w_ref.at[other], wa_ref.at[me], send.at[k], recv.at[k], other))
        copies[-1].start()
    wa_ref[me] = w_ref[me]
    for copy in copies:
        copy.wait()


def swap(w, collective_id):
    return pl.pallas_call(
        swap_kernel,
        out_shape=jax.ShapeDtypeStruct(w.shape, w.dtype),
        in_specs=[VM],
        out_specs=VM,
        scratch_shapes=[pltpu.SemaphoreType.DMA((3,))] * 2,
        compiler_params=params(collective_id),
        name="swap",
    )(w)


class Reduce:
    def __init__(self, p_ref, near, sent, far, send, recv):
        self.me, self.sib, self.opp, self.diag = places()
        self.refs = (p_ref, near, sent, far)
        self.part = part = p_ref.shape[1] // CHUNKS
        self.pieces = [pl.ds(k * part, part) for k in range(CHUNKS)]
        self.first, self.own, self.across = [], [], []
        for k, p in enumerate(self.pieces):
            self.first.append(push(p_ref.at[self.diag, p], near.at[0, p], send.at[k], recv.at[k], self.sib))
            self.own.append(push(p_ref.at[self.sib, p], near.at[1, p], send.at[CHUNKS + k], recv.at[CHUNKS + k], self.sib))
            self.across.append(push(sent.at[p], far.at[p], send.at[2 * CHUNKS + k], recv.at[2 * CHUNKS + k], self.opp))

    def start(self):
        p_ref, near, sent, far = self.refs
        for copy in self.first + self.own:
            copy.start()
        for k, p in enumerate(self.pieces):
            self.first[k].wait_recv()
            sent[p] = (p_ref[self.opp, p].astype(F32) + near[0, p].astype(F32)).astype(BF)
            self.across[k].start()

    def piece(self, k):
        p_ref, near, sent, far = self.refs
        p = self.pieces[k]
        self.own[k].wait_recv()
        self.across[k].wait_recv()
        return p_ref[self.me, p].astype(F32) + near[1, p].astype(F32) + far[p].astype(F32)

    def finish(self):
        for copy in self.first + self.own + self.across:
            copy.wait_send()


class Gather:
    def __init__(self, x_ref, all_ref, send, recv, base):
        self.me, self.sib, self.opp, self.diag = places()
        part = x_ref.shape[0] // CHUNKS
        self.pieces = [pl.ds(k * part, part) for k in range(CHUNKS)]
        self.across, self.near, self.onward = [], [], []
        me, sib, opp = self.me, self.sib, self.opp
        for k, p in enumerate(self.pieces):
            a, b, c = base + k, base + CHUNKS + k, base + 2 * CHUNKS + k
            self.across.append(push(x_ref.at[p], all_ref.at[me, p], send.at[a], recv.at[a], opp))
            self.near.append(push(x_ref.at[p], all_ref.at[me, p], send.at[b], recv.at[b], sib))
            self.onward.append(push(all_ref.at[opp, p], all_ref.at[opp, p], send.at[c], recv.at[c], sib))

    def start(self, k):
        self.across[k].start()
        self.near[k].start()

    def finish(self):
        for k in range(CHUNKS):
            self.across[k].wait_recv()
            self.onward[k].start()
        for copy in self.across:
            copy.wait_send()
        for copy in self.near + self.onward:
            copy.wait()


def normalise(values):
    centred = values - jnp.mean(values, axis=-1, keepdims=True)
    variance = jnp.mean(centred * centred, axis=-1, keepdims=True)
    scale = lax.rsqrt(variance + 1e-05)
    return centred * scale, scale


def norm_back(upstream, gain, unit, scale):
    inner = upstream * gain
    return scale * (
        inner
        - jnp.mean(inner, axis=-1, keepdims=True)
        - unit * jnp.mean(inner * unit, axis=-1, keepdims=True)
    )


def middle_kernel(p_ref, x_ref, vec_ref, r_ref, all_ref, near, sent, far, mine, send, recv):
    me, sib, opp, diag = places()
    greet(sib, opp)
    reduce = Reduce(p_ref, near, sent, far, send, recv)
    gather = Gather(mine, all_ref, send, recv, 3 * CHUNKS)
    reduce.start()
    for k, p in enumerate(reduce.pieces):
        r = x_ref[p].astype(F32) + (reduce.piece(k) + vec_ref[0:1])
        r_ref[p] = r
        unit, _ = normalise(r)
        low = (unit * vec_ref[1:2] + vec_ref[2:3]).astype(BF)
        mine[p] = low
        gather.start(k)
        all_ref[me, p] = low
    gather.finish()
    reduce.finish()


def reduce_scratch(rows, wide):
    return [
        pltpu.VMEM((2, rows, wide), BF),
        pltpu.VMEM((rows, wide), BF),
        pltpu.VMEM((rows, wide), BF),
    ]


def middle_step(p, x, vec):
    n, rows, wide = p.shape
    return pl.pallas_call(
        middle_kernel,
        out_shape=[
            jax.ShapeDtypeStruct((rows, wide), F32),
            jax.ShapeDtypeStruct((n, rows, wide), BF),
        ],
        in_specs=[VM] * 3,
        out_specs=[VM] * 2,
        scratch_shapes=reduce_scratch(rows, wide)
        + [pltpu.VMEM((rows, wide), BF)]
        + [pltpu.SemaphoreType.DMA((6 * CHUNKS,))] * 2,
        compiler_params=params(1),
        name="middle_step",
    )(p, x, vec)


def back_kernel(p_ref, r_ref, g_ref, vec_ref, gr_ref, all_ref, sums_ref, near, sent, far, mine, send, recv):
    me, sib, opp, diag = places()
    greet(sib, opp)
    reduce = Reduce(p_ref, near, sent, far, send, recv)
    gather = Gather(mine, all_ref, send, recv, 3 * CHUNKS)
    reduce.start()
    sums_ref[...] = jnp.zeros_like(sums_ref)
    for k, p in enumerate(reduce.pieces):
        unit, scale = normalise(r_ref[p])
        g = g_ref[p].astype(F32)
        upstream = reduce.piece(k)
        gr = g + norm_back(upstream, vec_ref[1:2], unit, scale)
        gr_ref[p] = gr
        low = gr.astype(BF)
        mine[p] = low
        gather.start(k)
        all_ref[me, p] = low
        sums_ref[0:1] += jnp.sum(upstream * unit, axis=0, keepdims=True)
        sums_ref[1:2] += jnp.sum(upstream, axis=0, keepdims=True)
        sums_ref[2:3] += jnp.sum(low.astype(F32), axis=0, keepdims=True)
        sums_ref[3:4] += jnp.sum(g, axis=0, keepdims=True)
    gather.finish()
    reduce.finish()


def back_step(p, r, g, vec):
    n, rows, wide = p.shape
    return pl.pallas_call(
        back_kernel,
        out_shape=[
            jax.ShapeDtypeStruct((rows, wide), F32),
            jax.ShapeDtypeStruct((n, rows, wide), BF),
            jax.ShapeDtypeStruct((8, wide), F32),
        ],
        in_specs=[VM] * 4,
        out_specs=[VM] * 3,
        scratch_shapes=reduce_scratch(rows, wide)
        + [pltpu.VMEM((rows, wide), BF)]
        + [pltpu.SemaphoreType.DMA((6 * CHUNKS,))] * 2,
        compiler_params=params(2),
        name="back_step",
    )(p, r, g, vec)


def last_kernel(p_ref, x_ref, r_ref, gr_ref, vec_ref, more_ref, y_ref, out_ref, sums_ref, near, sent, far, mine, send, recv):
    me, sib, opp, diag = places()
    greet(sib, opp, diag)
    reduce = Reduce(p_ref, near, sent, far, send, recv)
    reduce.start()
    wide = x_ref.shape[1]
    mine[...] = more_ref[...]
    for k, p in enumerate(reduce.pieces):
        unit, scale = normalise(x_ref[p].astype(F32))
        both = reduce.piece(k)
        y_ref[p] = (r_ref[p] + both[:, :wide] + vec_ref[1:2]).astype(BF)
        upstream = both[:, wide:]
        out_ref[p] = (gr_ref[p] + norm_back(upstream, vec_ref[0:1], unit, scale)).astype(BF)
        mine[0:1] += jnp.sum(upstream * unit, axis=0, keepdims=True)
        mine[1:2] += jnp.sum(upstream, axis=0, keepdims=True)
    copies = []
    for k, other in enumerate((opp, diag, sib)):
        slot = 3 * CHUNKS + k
        copies.append(push(mine, sums_ref.at[me], send.at[slot], recv.at[slot], other))
        copies[-1].start()
    sums_ref[me] = mine[...]
    for copy in copies:
        copy.wait()
    reduce.finish()


def last_step(p, x, r, gr, vec, more):
    n, rows, wide = p.shape
    return pl.pallas_call(
        last_kernel,
        out_shape=[
            jax.ShapeDtypeStruct(x.shape, BF),
            jax.ShapeDtypeStruct(x.shape, BF),
            jax.ShapeDtypeStruct((n,) + more.shape, F32),
        ],
        in_specs=[VM] * 6,
        out_specs=[VM] * 3,
        scratch_shapes=reduce_scratch(rows, wide)
        + [pltpu.VMEM(more.shape, F32)]
        + [pltpu.SemaphoreType.DMA((3 * CHUNKS + 3,))] * 2,
        compiler_params=params(3),
        name="last_step",
    )(p, x, r, gr, vec, more)


def head_mask(wide):
    lane = lax.broadcasted_iota(jnp.int32, (1, wide), 1)
    low = pl.program_id(0) * HD
    return (lane >= low) & (lane < low + HD)


def causal(block, first, count):
    row = lax.broadcasted_iota(jnp.int32, (block, count), 0) + first
    return row >= lax.broadcasted_iota(jnp.int32, (block, count), 1)


def attend_kernel(block, q_ref, k_ref, v_ref, o_ref, lse_ref):
    length, wide = q_ref.shape
    mask = head_mask(wide)
    for first in range(0, length, block):
        count = first + block
        rows = slice(first, count)
        q = jnp.where(mask, q_ref[rows], 0) * BF(HD**-0.5)
        s = jnp.where(causal(block, first, count), along_rows(q, k_ref[:count]), -1e30)
        top = jnp.max(s, axis=-1, keepdims=True)
        p = jnp.exp(s - top)
        total = jnp.sum(p, axis=-1, keepdims=True)
        o = jnp.dot(p.astype(BF), v_ref[:count], preferred_element_type=F32) / total
        o_ref[rows] = jnp.where(mask, o.astype(BF), o_ref[rows])
        lse_ref[0, rows] = jnp.broadcast_to(top + jnp.log(total), (block, 128))


def attend(q, k, v):
    length, wide = q.shape
    heads = wide // HD
    whole = pl.BlockSpec((length, wide), lambda h: (0, 0))
    return pl.pallas_call(
        partial(attend_kernel, min(256, length)),
        grid=(heads,),
        out_shape=[
            jax.ShapeDtypeStruct((length, wide), BF),
            jax.ShapeDtypeStruct((heads, length, 128), F32),
        ],
        in_specs=[whole] * 3,
        out_specs=[whole, pl.BlockSpec((1, length, 128), lambda h: (h, 0, 0))],
        compiler_params=params(),
        cost_estimate=pl.CostEstimate(flops=4 * heads * length * length * 256, bytes_accessed=8 * length * wide, transcendentals=heads * length * length),
        name="attend",
    )(q, k, v)


def attend_back_kernel(block, q_ref, k_ref, v_ref, go_ref, lse_ref, gq_ref, gk_ref, gv_ref, gk_sum, gv_sum):
    length, wide = q_ref.shape
    mask = head_mask(wide)

    @pl.when(pl.program_id(0) == 0)
    def _():
        gk_sum[...] = jnp.zeros_like(gk_sum)
        gv_sum[...] = jnp.zeros_like(gv_sum)

    for first in range(0, length, block):
        count = first + block
        rows = slice(first, count)
        q = jnp.where(mask, q_ref[rows], 0) * BF(HD**-0.5)
        go = jnp.where(mask, go_ref[rows], 0)
        s = along_rows(q, k_ref[:count])
        p = jnp.where(causal(block, first, count), jnp.exp(s - lse_ref[0, rows, 0:1]), 0.0)
        dp = along_rows(go, v_ref[:count])
        delta = jnp.sum(p * dp, axis=-1, keepdims=True)
        ds = (p * (dp - delta)).astype(BF)
        gq = jnp.dot(ds, k_ref[:count], preferred_element_type=F32) * HD**-0.5
        gq_ref[rows] = jnp.where(mask, gq.astype(BF), gq_ref[rows])
        gk_sum[:count] += across_rows(ds, q)
        gv_sum[:count] += across_rows(p.astype(BF), go)

    @pl.when(pl.program_id(0) == pl.num_programs(0) - 1)
    def _():
        gk_ref[...] = gk_sum[...].astype(BF)
        gv_ref[...] = gv_sum[...].astype(BF)


def attend_back(q, k, v, go, lse):
    length, wide = q.shape
    heads = wide // HD
    whole = pl.BlockSpec((length, wide), lambda h: (0, 0))
    return pl.pallas_call(
        partial(attend_back_kernel, min(256, length)),
        grid=(heads,),
        out_shape=[jax.ShapeDtypeStruct((length, wide), BF)] * 3,
        in_specs=[whole] * 4 + [pl.BlockSpec((1, length, 128), lambda h: (h, 0, 0))],
        out_specs=[whole] * 3,
        scratch_shapes=[pltpu.VMEM((length, wide), F32)] * 2,
        compiler_params=params(),
        cost_estimate=pl.CostEstimate(flops=10 * heads * length * length * 256, bytes_accessed=16 * length * wide, transcendentals=heads * length * length),
        name="attend_back",
    )(q, k, v, go, lse)


def turn(blocks, n):
    me = lax.axis_index("cp")
    result = jnp.zeros_like(blocks)
    result = lax.dynamic_update_index_in_dim(result, lax.dynamic_index_in_dim(blocks, me, 0), me, 0)
    for step in range(1, n):
        there, back = lax.rem(me + step, n), lax.rem(me + n - step, n)
        got = lax.ppermute(
            lax.dynamic_index_in_dim(blocks, there, 0), "cp", [(i, (i + step) % n) for i in range(n)]
        )
        result = lax.dynamic_update_index_in_dim(result, got, back, 0)
    return result


def head_body(
    tokens, cotangent, ln1_gain, ln1_bias, w_qkv, b_qv, w_out, b_out,
    ln2_gain, ln2_bias, w_in, b_in, w_down, b_down, *, n,
):
    rows = tokens.shape[0]
    length = rows * n
    me = lax.axis_index("cp")
    share = D // n
    ff_share = w_in.shape[1] // n
    tidy = jnp.concatenate([ln1_gain, ln1_bias, b_out, ln2_gain, ln2_bias, b_down, b_qv])
    tidy = jnp.concatenate([tidy, jnp.zeros((-tidy.shape[0] % 2048,), BF)]).reshape(-1, 128)
    w_blocks = w_qkv.reshape(share, 3, n, share).transpose(2, 0, 1, 3).reshape(n, share, 3 * share)
    x_all, w_mine, tidy_all = open_exchange(tokens, w_blocks, tidy)
    x_all, late_in, late_cot = lax.optimization_barrier((x_all, w_in, cotangent))
    in_cols = turn(late_in.reshape(share, n, ff_share).transpose(1, 0, 2), n).reshape(D, ff_share)
    cot_all = lax.all_gather(late_cot, "cp", axis=0, tiled=True)
    w_mine = w_mine.reshape(D, 3 * share)
    tidy_all = tidy_all.reshape(n, -1).astype(F32)
    gain_one, shift_one, out_bias, gain_two, shift_two, down_bias = (
        tidy_all[:, i * share : (i + 1) * share].reshape(D) for i in range(6)
    )
    qv_bias = tidy_all[:, 6 * share : 8 * share].reshape(2, D)
    qv_mine = lax.dynamic_slice_in_dim(qv_bias, me * share, share, 1)
    vec_two = jnp.concatenate([jnp.stack([out_bias, gain_two, shift_two]), jnp.zeros((5, D), F32)])
    vec_one = jnp.concatenate([jnp.stack([gain_one, down_bias]), jnp.zeros((6, D), F32)])

    n1 = layer_norm(x_all.reshape(length, D).astype(F32), gain_one, shift_one).astype(BF)
    mixed = jnp.dot(n1, w_mine, preferred_element_type=F32)
    q = (mixed[:, :share] + qv_mine[0]).astype(BF)
    k = mixed[:, share : 2 * share].astype(BF)
    v = (mixed[:, 2 * share :] + qv_mine[1]).astype(BF)
    o, lse = attend(q, k, v)
    o_part = jnp.dot(o, w_out, preferred_element_type=F32).astype(BF).reshape(n, rows, D)
    r, n2 = middle_step(o_part, tokens, vec_two)
    n2 = n2.reshape(length, D)
    hidden = jnp.dot(n2, in_cols, preferred_element_type=F32) + b_in.astype(F32)
    active, gelu_back = jax.vjp(partial(jax.nn.gelu, approximate=True), hidden)
    a = active.astype(BF)
    y_part = jnp.dot(a, w_down, preferred_element_type=F32).astype(BF)
    gu = gelu_back(along_rows(cot_all, w_down))[0].astype(BF)
    n2_part = along_rows(gu, in_cols).astype(BF).reshape(n, rows, D)
    grad_down = across_rows(a, cot_all).astype(BF)
    grad_in = across_rows(n2, gu).astype(BF).reshape(n, share, ff_share)
    grad_in_bias = jnp.sum(gu.astype(F32), axis=0)
    n2_part, grad_down, grad_in = lax.optimization_barrier((n2_part, grad_down, grad_in))
    grad_down, grad_in = lax.psum((grad_down, grad_in), "rep")

    gr, gz, sums_two = back_step(n2_part, r, cotangent, vec_two)
    gz = gz.reshape(length, D)
    go = along_rows(gz, w_out).astype(BF)
    grad_out = across_rows(o, gz).astype(BF)
    gq, gk, gv = attend_back(q, k, v, go, lse)
    gm = jnp.concatenate([gq, gk, gv], axis=1)
    grad_qkv = swap(across_rows(n1, gm).astype(BF).reshape(n, share, 3 * share), 4)
    grad_qkv = grad_qkv.reshape(n, share, 3, share).transpose(1, 2, 0, 3).reshape(share, 3 * D)
    n1_part = along_rows(gm, w_mine).astype(BF)
    both_parts = jnp.concatenate([y_part, n1_part], axis=1).reshape(n, rows, 2 * D)

    qv_sums = jnp.zeros((2, D), F32)
    qv_sums = lax.dynamic_update_slice(
        qv_sums,
        jnp.stack([jnp.sum(gq.astype(F32), axis=0), jnp.sum(gv.astype(F32), axis=0)]),
        (0, me * share),
    )
    in_sums = lax.dynamic_update_slice(jnp.zeros((n * ff_share,), F32), grad_in_bias, (me * ff_share,))
    more = jnp.concatenate(
        [jnp.zeros((2, D), F32), sums_two[:4], qv_sums, in_sums.reshape(-1, D), jnp.zeros((4, D), F32)]
    )
    layer_out, input_grad, sums_all = last_step(both_parts, tokens, r, gr, vec_one, more)
    sums = jnp.sum(sums_all, axis=0)
    own = lax.dynamic_slice_in_dim(sums[:6], me * share, share, 1)
    own_qv = lax.dynamic_slice_in_dim(sums[6:8].reshape(-1), me * 2 * share, 2 * share, 0)
    own_in = lax.dynamic_slice_in_dim(sums[8:12].reshape(-1), me * ff_share, ff_share, 0)
    small = jnp.concatenate([own.reshape(-1), own_qv, own_in]).astype(BF).reshape(-1, 128)
    small, grad_qkv, grad_out, grad_down, grad_in = lax.optimization_barrier(
        (small, grad_qkv, grad_out, grad_down, grad_in)
    )
    grad_qkv, grad_out, small = lax.psum((grad_qkv, grad_out, small), "rep")
    grad_in = swap(grad_in, 5).transpose(1, 0, 2).reshape(share, n * ff_share).astype(F32)
    grad_down, grad_qkv, grad_out = (item.astype(F32) for item in (grad_down, grad_qkv, grad_out))
    small = small.astype(F32).reshape(-1)
    own = small[: 6 * share].reshape(6, share)
    own_qv = small[6 * share : 8 * share]
    own_in = small[8 * share :]
    return (
        layer_out, input_grad, own[0], own[1], grad_qkv, own_qv, grad_out, own[4],
        own[2], own[3], grad_in, own_in, grad_down, own[5],
    )


def solution(mesh):
    placed = (
        P(("rep", "cp"), None),
        P(("rep", "cp"), None),
        P("cp"),
        P("cp"),
        P("cp", None),
        P("cp"),
        P("cp", None),
        P("cp"),
        P("cp"),
        P("cp"),
        P("cp", None),
        P("cp"),
        P("cp", None),
        P("cp"),
    )
    count = mesh.shape["cp"]
    by_heads = count == 4 and H % count == 0
    return jax.shard_map(
        partial(head_body, n=count) if by_heads else body,
        mesh=mesh,
        in_specs=placed,
        out_specs=(
            P(("rep", "cp"), None),
            P(("rep", "cp"), None),
            P("cp"),
            P("cp"),
            P("cp", None),
            P("cp"),
            P("cp", None),
            P("cp"),
            P("cp"),
            P("cp"),
            P("cp", None),
            P("cp"),
            P("cp", None),
            P("cp"),
        ),
        check_vma=False,
    )
```
